128 devices in a mesh: ep: 32 (over x, y, core), th: 4 (over z).
Axes of the slice: x: 4, y: 4, z: 4, core: 2. Of those that a mesh axis runs over, the one named last changes fastest.
Arguments:
- tokens: bfloat16 [4096, 4096], P('ep', 'th'), may hold values from -6 to 6
- cotangent: bfloat16 [4096, 4096], P('ep', 'th'), may hold values from -6 to 6
- gates: bfloat16 [4096, 8], P('ep'), may hold values from 0.049804688 to 0.5
- routing: int32 [4096, 8], P('ep'), may hold values from 0 to 31, all different within a row; in each aligned block of 128 rows (0 to 127, 128 to 255, ...) at most 36 rows name the same one
- new_slot: int32 [32], replicated, may hold values from 0 to 31, each once
- gate_old: bfloat16 [32, 4096, 1536], P(None, 'ep', 'th'), may hold values from -0.09375 to 0.09375
- up_old: bfloat16 [32, 4096, 1536], P(None, 'ep', 'th'), may hold values from -0.09375 to 0.09375
- down_old: bfloat16 [32, 4096, 1536], P(None, 'ep', 'th'), may hold values from -0.15625 to 0.15625
Outputs:
- grad_tokens: bfloat16 [4096, 4096], P('ep', 'th')
- grad_gates: bfloat16 [4096, 8], P('ep')
- grad_gate_w: bfloat16 [32, 4096, 1536], P('ep', None, 'th')
- grad_up_w: bfloat16 [32, 4096, 1536], P('ep', None, 'th')
- grad_down_w: bfloat16 [32, 4096, 1536], P('ep', None, 'th')
The draws below stay inside these ranges and needn't reach their ends.
Inputs may be any that keep to these rules, and one draw needn't show every extreme that they name: `routing`: each row names 8 different experts; among the rows of one device (128 aligned rows) no expert is named by more than 36 rows, and one expert is named by exactly 36 in some blocks. `new_slot`: each compacted id stands once.
All inputs are finite; a program needn't handle non-finite values.
Results may differ from the reference program's by a relative error of at most 0.015.
Values may be sent and summed in bfloat16 or wider, within the bound.
A program may use at most 192 MiB of HBM per device.

```python
import math
import jax
import jax.numpy as jnp
import numpy as np
from jax import lax

D = 4096
FF = 1536
TOP = 8
EXPERTS = 32
TOK_DEV = 128
CAP = 36
TOKENS = 4096
N_EP = 32
N_TH = 4


def block_levels(own_key, extent, shards, least, largest):
    loudness = 1.0
    for axis_at, blocks in shards:
        heights = jax.random.uniform(jax.random.fold_in(jax.random.fold_in(own_key, 6), axis_at), (blocks,), jnp.float32, least / len(shards), largest / len(shards))
        loudness = loudness * jnp.repeat(jnp.exp(heights), extent[axis_at] // blocks).reshape((-1,) + (1,) * (len(extent) - 1 - axis_at))
    return loudness


def shared_out(rng, own, number, rows, amount, top, limit, slope):
    sequence = jax.random.permutation(rng, amount)
    crowded, ordinary = load_shares(amount, rows * top, limit, slope, True), load_shares(amount, rows * top, limit, slope, False)
    places = jnp.arange(amount)

    def named(sizes, turn):
        used = int((sizes > 0).sum())
        fixed = max(1, used // 4)
        passed = fixed + (places - fixed + turn * (used - fixed)) % max(1, amount - fixed)
        return jnp.zeros((amount,), jnp.int32).at[sequence[jnp.where(places < fixed, places, passed)]].set(jnp.asarray(sizes, jnp.int32))

    sizes = jnp.where(number % 4 == 0, named(crowded, number // 4), named(ordinary, number - number // 4 - 1))
    mixed = jax.random.permutation(jax.random.fold_in(own, 3), amount)
    giver, receiver = mixed[0:amount // 2 * 2:2], mixed[1:amount // 2 * 2:2]
    margin = jnp.minimum(sizes[giver] - 1, limit - sizes[receiver]) // 2
    margin = jnp.where((giver == sequence[0]) | (receiver == sequence[0]) | (sizes[receiver] == 0), 0, jnp.maximum(margin, 0))
    passed = jax.random.randint(jax.random.fold_in(own, 4), (amount // 2,), 0, 1 << 20) % (margin + 1)
    sizes = sizes.at[giver].add(-passed).at[receiver].add(passed)
    labels = jnp.searchsorted(jnp.cumsum(sizes), jnp.arange(rows * top), side="right").astype(jnp.int32)
    grid = labels.reshape(top, rows).T
    grid = grid[jax.random.permutation(jax.random.fold_in(own, 1), rows)]
    turn = jax.random.randint(jax.random.fold_in(own, 2), (rows, 1), 0, top)
    return jnp.take_along_axis(grid, (jnp.arange(top)[None, :] + turn) % top, axis=1)


def load_shares(count, total, bound, skew, full):
    loads = [(1 << 20) // math.isqrt(grade ** skew) + 1 for grade in range(1, count + 1)]
    largest = bound if full else min(bound, max(-(-total // count), total * loads[0] // sum(loads)))
    least = 1 if total - largest >= count - 1 else 0
    counts, rest = [largest] + [least] * (count - 1), total - largest - least * (count - 1)
    while rest > 0:
        free = [i for i in range(1, count) if counts[i] < largest] or [i for i in range(1, count) if counts[i] < bound]
        whole, left = sum([loads[i] for i in free]), rest
        for i in free:
            extra = min(bound - counts[i], max(1, left * loads[i] // whole), rest)
            counts[i] = counts[i] + extra
            rest = rest - extra
    return np.array(counts)


def bell_draw(key, extent, deviation, limit, cuts=(), kind=jnp.bfloat16):
    values = deviation * jax.random.normal(key, extent, jnp.float32)
    if cuts:
        values = values * block_levels(key, extent, cuts, -0.22, 0.18)
    return jnp.clip(values, -limit, limit).astype(kind)


def setup_inputs(seed: int = 0) -> dict:
    seeds = jax.random.split(jax.random.key(seed), 9)
    tokens = bell_draw(seeds[0], (TOKENS, D), 1.0, 6.0, ((0, 32), (1, 4)))
    cotangent = bell_draw(seeds[1], (TOKENS, D), 1.0, 6.0, ((0, 32), (1, 4)))
    gates = jnp.clip(jnp.exp(math.log(0.5) - 2.306499 * jax.random.uniform(seeds[2], (TOKENS, TOP), jnp.float32) ** block_levels(seeds[2], (TOKENS, TOP), ((0, 32),), -0.2, 0.2)), 0.049804688, 0.5).astype(jnp.bfloat16)
    routing_keys = jax.random.split(jax.random.fold_in(seeds[3], 1), TOKENS // TOK_DEV)
    routing_turns = jax.random.permutation(jax.random.fold_in(seeds[3], 3), TOKENS // TOK_DEV)
    routing = jax.vmap(lambda own, number: shared_out(jax.random.fold_in(seeds[3], 2), own, number, TOK_DEV, EXPERTS, TOP, CAP, 1))(routing_keys, routing_turns).reshape((TOKENS, TOP))
    new_slot = jax.random.permutation(seeds[4], EXPERTS).astype(jnp.int32)
    gate_old = bell_draw(seeds[5], (EXPERTS, D, FF), D ** -0.5, 0.09375, ((1, 32), (2, 4)))
    up_old = bell_draw(seeds[6], (EXPERTS, D, FF), D ** -0.5, 0.09375, ((1, 32), (2, 4)))
    down_old = bell_draw(seeds[7], (EXPERTS, D, FF), FF ** -0.5, 0.15625, ((1, 32), (2, 4)))
    return {"tokens": tokens, "cotangent": cotangent, "gates": gates, "routing": routing, "new_slot": new_slot, "gate_old": gate_old, "up_old": up_old, "down_old": down_old}


def slot_ranks(route_rows, expert_ids):
    hit_table = (route_rows[:, None] == expert_ids[None, :]).astype(jnp.int32)
    earlier = jnp.cumsum(hit_table, axis=0) - hit_table
    return jnp.sum(earlier * hit_table, axis=1).astype(jnp.int32)


def reference(tokens, cotangent, gates, routing, new_slot, gate_old, up_old, down_old):
    expert_ids = jnp.arange(EXPERTS, dtype=jnp.int32)
    hit_map = (new_slot[None, :] == expert_ids[:, None]).astype(jnp.int32)
    inverse = jnp.sum(hit_map * expert_ids[None, :], axis=1).astype(jnp.int32)
    per_block = TOK_DEV * TOP
    blocks = routing.reshape(N_EP, per_block)
    ranks = jax.vmap(lambda rows: slot_ranks(rows, expert_ids))(blocks)
    entries = jnp.arange(N_EP * per_block, dtype=jnp.int32).reshape(N_EP, per_block)
    sources = entries // per_block
    table = jnp.full((EXPERTS, N_EP, CAP), -1, jnp.int32).at[blocks, sources, ranks].set(entries)
    gate_flat = gates.reshape(-1)
    group = FF // N_TH

    def one_expert(expert):
        entry_index = table[expert].reshape(-1)
        valid = entry_index >= 0
        safe_entry = jnp.maximum(entry_index, 0)
        token_index = safe_entry // TOP
        live = valid[:, None].astype(jnp.bfloat16)
        rows_in = tokens[token_index] * live
        rows_grad = cotangent[token_index] * live
        weight_g = (gate_flat[safe_entry].astype(jnp.float32) * valid.astype(jnp.float32))[:, None]
        old_index = inverse[expert]
        w_gate = gate_old[old_index]
        w_up = up_old[old_index]
        w_down = down_old[old_index]
        gate_pre = jnp.dot(rows_in, w_gate, preferred_element_type=jnp.float32)
        up_pre = jnp.dot(rows_in, w_up, preferred_element_type=jnp.float32)
        back_hid = jnp.dot(rows_grad, w_down, preferred_element_type=jnp.float32)
        sigmoid_gate = jax.nn.sigmoid(gate_pre)
        silu_gate = gate_pre * sigmoid_gate
        hidden = silu_gate * up_pre
        grad_hid = weight_g * back_hid
        grad_gate_pre = (grad_hid * up_pre * sigmoid_gate * (1.0 + gate_pre * (1.0 - sigmoid_gate))).astype(jnp.bfloat16)
        grad_up_pre = (grad_hid * silu_gate).astype(jnp.bfloat16)
        scaled_hidden = (weight_g * hidden).astype(jnp.bfloat16)
        router_term = jnp.sum(back_hid * hidden, axis=1).astype(jnp.bfloat16)
        grad_wg = jnp.dot(rows_in.T, grad_gate_pre, preferred_element_type=jnp.float32).astype(jnp.bfloat16)
        grad_wu = jnp.dot(rows_in.T, grad_up_pre, preferred_element_type=jnp.float32).astype(jnp.bfloat16)
        grad_wd = jnp.dot(rows_grad.T, scaled_hidden, preferred_element_type=jnp.float32).astype(jnp.bfloat16)
        total = jnp.zeros((rows_in.shape[0], D), jnp.float32)
        for part in range(N_TH):
            start = part * group
            term = jnp.dot(grad_gate_pre[:, start:start + group], w_gate[:, start:start + group].T, preferred_element_type=jnp.float32)
            term = term + jnp.dot(grad_up_pre[:, start:start + group], w_up[:, start:start + group].T, preferred_element_type=jnp.float32)
            total = total + lax.optimization_barrier(term.astype(jnp.bfloat16)).astype(jnp.float32)
        slot_grad = total.astype(jnp.bfloat16)
        return grad_wg, grad_wu, grad_wd, slot_grad, router_term

    grad_gate_w, grad_up_w, grad_down_w, slot_grads, router_terms = lax.map(one_expert, expert_ids)
    all_entries = table.reshape(-1)
    valid_all = all_entries >= 0
    token_target = jnp.where(valid_all, all_entries // TOP, TOKENS).astype(jnp.int32)
    grad_tokens = jnp.zeros((TOKENS, D), jnp.float32).at[token_target].add(slot_grads.reshape(-1, D).astype(jnp.float32), mode="drop")
    entry_target = jnp.where(valid_all, all_entries, TOKENS * TOP).astype(jnp.int32)
    grad_gates = jnp.zeros((TOKENS * TOP,), jnp.float32).at[entry_target].set(router_terms.reshape(-1).astype(jnp.float32), mode="drop")
    return (grad_tokens.astype(jnp.bfloat16), grad_gates.reshape(TOKENS, TOP).astype(jnp.bfloat16), grad_gate_w, grad_up_w, grad_down_w)
```

```python
import jax
import jax.numpy as jnp
from jax import lax
from jax.experimental import pallas as pl
from jax.experimental.pallas import tpu as pltpu
from jax.sharding import PartitionSpec as P

CAP = 36


def reorder_body(inverse, gate_ref, up_ref, down_ref, gate_out, up_out, down_out):
    del inverse
    gate_out[...] = gate_ref[...]
    up_out[...] = up_ref[...]
    down_out[...] = down_ref[...]


def reorder(inverse, gate_old, up_old, down_old):
    count, rows, cols = gate_old.shape
    read = pl.BlockSpec((1, rows, cols), lambda j, inv: (inv[j], 0, 0))
    write = pl.BlockSpec((1, rows, cols), lambda j, inv: (j, 0, 0))
    return pl.pallas_call(
        reorder_body,
        out_shape=[jax.ShapeDtypeStruct(gate_old.shape, gate_old.dtype)] * 3,
        grid_spec=pltpu.PrefetchScalarGridSpec(
            num_scalar_prefetch=1, grid=(count,), in_specs=[read] * 3, out_specs=[write] * 3
        ),
    )(inverse, gate_old, up_old, down_old)


def local(tokens, cotangent, gates, routing, new_slot, gate_old, up_old, down_old):
    expert_total = new_slot.shape[0]
    tok_count, top_count = routing.shape
    expert_ids = jnp.arange(expert_total, dtype=jnp.int32)
    inverse = jnp.sum(
        (new_slot[None, :] == expert_ids[:, None]).astype(jnp.int32) * expert_ids[None, :], axis=1
    )
    w_gate, w_up, w_down = (
        lax.all_to_all(w, "ep", split_axis=0, concat_axis=1, tiled=True)[0]
        for w in reorder(inverse, gate_old, up_old, down_old)
    )
    named = routing[:, :, None] == expert_ids[None, None, :]
    hits = jnp.any(named, axis=1)
    order = jnp.arange(tok_count, dtype=jnp.int32)
    below = (order[:, None] > order[None, :]).astype(jnp.bfloat16)
    rank = jnp.dot(below, hits.astype(jnp.bfloat16), preferred_element_type=jnp.float32)
    place = jnp.where(hits, rank, -1.0).astype(jnp.int32)
    ranks = jnp.arange(CAP, dtype=jnp.int32)
    pick = (place.T[:, None, :] == ranks[None, :, None]).astype(jnp.bfloat16)
    pick = pick.reshape(expert_total * CAP, tok_count)
    gate_of = jnp.sum(jnp.where(named, gates.astype(jnp.float32)[:, :, None], 0.0), axis=1)
    gate_send = jnp.sum(
        pick.reshape(expert_total, CAP, tok_count).astype(jnp.float32) * gate_of.T[:, None, :],
        axis=2,
    ).reshape(-1)
    both = jnp.concatenate([tokens, cotangent], axis=1)
    rows_send = jnp.dot(pick, both, preferred_element_type=jnp.float32).astype(jnp.bfloat16)
    rows_quarter = lax.all_to_all(rows_send, "ep", split_axis=0, concat_axis=0, tiled=True)
    weight_g = lax.all_to_all(gate_send, "ep", split_axis=0, concat_axis=0, tiled=True)[:, None]
    quarter = tokens.shape[1]
    rows_in = lax.all_gather(rows_quarter[:, :quarter], "th", axis=1, tiled=True)
    rows_grad = lax.all_gather(rows_quarter[:, quarter:], "th", axis=1, tiled=True)
    gate_pre = jnp.dot(rows_in, w_gate, preferred_element_type=jnp.float32)
    up_pre = jnp.dot(rows_in, w_up, preferred_element_type=jnp.float32)
    back_hid = jnp.dot(rows_grad, w_down, preferred_element_type=jnp.float32)
    sigmoid_gate = jax.nn.sigmoid(gate_pre)
    silu_gate = gate_pre * sigmoid_gate
    hidden = silu_gate * up_pre
    grad_hid = weight_g * back_hid
    grad_gate_pre = (
        grad_hid * up_pre * sigmoid_gate * (1.0 + gate_pre * (1.0 - sigmoid_gate))
    ).astype(jnp.bfloat16)
    grad_up_pre = (grad_hid * silu_gate).astype(jnp.bfloat16)
    scaled_hidden = (weight_g * hidden).astype(jnp.bfloat16)
    router_part = jnp.sum(back_hid * hidden, axis=1)
    over_rows = (((0,), (0,)), ((), ()))
    grad_wg, grad_wu, grad_wd = (
        lax.dot_general(a, b, over_rows, preferred_element_type=jnp.float32).astype(jnp.bfloat16)[
            None
        ]
        for a, b in (
            (rows_in, grad_gate_pre),
            (rows_in, grad_up_pre),
            (rows_grad, scaled_hidden),
        )
    )
    over_hidden = (((1,), (1,)), ((), ()))
    partial_value = lax.dot_general(
        grad_gate_pre, w_gate, over_hidden, preferred_element_type=jnp.float32
    ) + lax.dot_general(grad_up_pre, w_up, over_hidden, preferred_element_type=jnp.float32)
    slot_grad = lax.psum_scatter(
        partial_value.astype(jnp.bfloat16), "th", scatter_dimension=1, tiled=True
    )
    router_term = lax.psum(router_part, "th").astype(jnp.bfloat16)
    back_rows = lax.all_to_all(slot_grad, "ep", split_axis=0, concat_axis=0, tiled=True)
    back_router = lax.all_to_all(router_term, "ep", split_axis=0, concat_axis=0, tiled=True)
    grad_tokens = lax.dot_general(
        pick, back_rows, over_rows, preferred_element_type=jnp.float32
    ).astype(jnp.bfloat16)
    router_of = jnp.sum(
        (pick.astype(jnp.float32) * back_router.astype(jnp.float32)[:, None]).reshape(
            expert_total, CAP, tok_count
        ),
        axis=1,
    ).T
    grad_gates = jnp.sum(jnp.where(named, router_of[:, None, :], 0.0), axis=2)
    return (grad_tokens, grad_gates.astype(jnp.bfloat16), grad_wg, grad_wu, grad_wd)


def solution(mesh):
    placed = (
        P("ep", "th"),
        P("ep", "th"),
        P("ep", None),
        P("ep", None),
        P(),
        P(None, "ep", "th"),
        P(None, "ep", "th"),
        P(None, "ep", "th"),
    )
    return jax.shard_map(
        local,
        mesh=mesh,
        in_specs=placed,
        out_specs=(
            P("ep", "th"),
            P("ep", None),
            P("ep", None, "th"),
            P("ep", None, "th"),
            P("ep", None, "th"),
        ),
        check_vma=False,
    )
```

```python
import jax
import jax.numpy as jnp
from jax import lax
from jax.experimental import pallas as pl
from jax.experimental.pallas import tpu as pltpu
from jax.sharding import PartitionSpec as P

CAP = 36
PEERS = 32
SET = 4
CHUNKS = 4
SETS = PEERS // SET
PER = SETS // CHUNKS
SROWS = SET * CAP
CROWS = PER * SROWS
MESH = pl.DeviceIdType.MESH
F32 = jnp.float32
BF16 = jnp.bfloat16


def offset(k):
    m = k // 2
    return m % 4, (m // 4 + m % 4) % 4, k % 2


def peer_to(me, k):
    dx, dy, dc = offset(k)
    return (me // 8 + dx) % 4 * 8 + ((me // 2) % 4 + dy) % 4 * 2 + (me % 2 + dc) % 2


def peer_from(me, k):
    dx, dy, dc = offset(k)
    return (me // 8 + 4 - dx) % 4 * 8 + ((me // 2) % 4 + 4 - dy) % 4 * 2 + (me % 2 + dc) % 2


def reorder_body(order, gate_ref, up_ref, down_ref, out_ref, held, in_sems, out_sems):
    depth = gate_ref.shape[1]

    def reads(k):
        return [
            pltpu.make_async_copy(
                ref.at[order[k]], held.at[k, pl.ds(n * depth, depth)], in_sems.at[n, k]
            )
            for n, ref in enumerate((gate_ref, up_ref, down_ref))
        ]

    def write(k):
        return pltpu.make_async_copy(held.at[k], out_ref.at[k], out_sems.at[k])

    @pl.loop(0, PEERS)
    def _(k):
        for copy in reads(k):
            copy.start()

    @pl.loop(0, PEERS)
    def _(k):
        for copy in reads(k):
            copy.wait()
        write(k).start()

    @pl.loop(0, PEERS)
    def _(k):
        write(k).wait()


def reorder(order, gate_old, up_old, down_old):
    count, depth, cols = gate_old.shape
    return pl.pallas_call(
        reorder_body,
        out_shape=jax.ShapeDtypeStruct((count, 3 * depth, cols), gate_old.dtype),
        grid_spec=pltpu.PrefetchScalarGridSpec(
            num_scalar_prefetch=1,
            grid=(),
            in_specs=[pl.BlockSpec(memory_space=pl.ANY)] * 3,
            out_specs=pl.BlockSpec(memory_space=pl.ANY),
            scratch_shapes=[
                pltpu.VMEM((count, 3 * depth, cols), gate_old.dtype),
                pltpu.SemaphoreType.DMA((3, count)),
                pltpu.SemaphoreType.DMA((count,)),
            ],
        ),
        compiler_params=pltpu.CompilerParams(vmem_limit_bytes=24 * 2**20),
    )(order, gate_old, up_old, down_old)


def layer_body(
    rows_ref, gsend_ref, wsend_ref, pack_ref, packt_ref,
    gw_ref, back_ref, qback_ref,
    wv, xy, rr, gr, dab, acc, s1s, s1r, s2s, s2r, own, ret, qp, qr, qs, stage,
    row_s, row_r, g_s, g_r, w_s, w_r, z_s, z_r, v_s, v_r, s1_s, s1_r, s2_s, s2_r,
    b_s, b_r, q_s, q_r, qb_s, qb_r, o_s,
):
    me = lax.axis_index("ep")
    th = lax.axis_index("th")
    right, left, opp = (th + 1) % 4, (th + 3) % 4, (th + 2) % 4
    cols = wv.shape[2]

    def ep_copy(src, dst, s, r, p):
        return pltpu.make_async_remote_copy(
            src_ref=src, dst_ref=dst, send_sem=s, recv_sem=r, device_id={"ep": p},
            device_id_type=MESH,
        )

    def th_copy(src, dst, s, r, p):
        return pltpu.make_async_remote_copy(
            src_ref=src, dst_ref=dst, send_sem=s, recv_sem=r, device_id={"th": p},
            device_id_type=MESH,
        )

    barrier = pltpu.get_barrier_semaphore()

    @pl.loop(1, PEERS)
    def _(k):
        pl.semaphore_signal(
            barrier, inc=1, device_id={"ep": peer_to(me, k)}, device_id_type=MESH
        )

    for p in (right, left, opp):
        pl.semaphore_signal(barrier, inc=1, device_id={"th": p}, device_id_type=MESH)
    pl.semaphore_wait(barrier, PEERS - 1 + 3)

    def row_copy(k):
        return ep_copy(rows_ref.at[k], rr.at[k], row_s.at[k], row_r.at[k], peer_to(me, k))

    def g_copy(k):
        return ep_copy(gsend_ref.at[k], gr.at[k], g_s.at[k], g_r.at[k], peer_to(me, k))

    def w_copy(k):
        return ep_copy(wsend_ref.at[k], wv.at[me], w_s.at[k], w_r.at[k], peer_to(me, k))

    def w_wait(k):
        s = peer_from(me, k)
        ep_copy(wsend_ref.at[k], wv.at[s], w_s.at[k], w_r.at[k], s).wait_recv()

    row_own = pltpu.make_async_copy(rows_ref.at[0], rr.at[0], row_r.at[0])
    g_own = pltpu.make_async_copy(gsend_ref.at[0], gr.at[0], g_r.at[0])
    w_own = pltpu.make_async_copy(wsend_ref.at[0], wv.at[me], w_r.at[0])
    row_own.start()
    g_own.start()

    @pl.loop(1, PEERS)
    def _(k):
        g_copy(k).start()
        row_copy(k).start()

    w_own.start()

    @pl.loop(1, PEERS)
    def _(k):
        w_copy(k).start()

    def z_copies(i):
        return (
            th_copy(xy.at[th, i], xy.at[th, i], z_s.at[0, i], z_r.at[0, i], right),
            th_copy(xy.at[th, i], xy.at[th, i], z_s.at[1, i], z_r.at[1, i], left),
        )

    def z_wait(i):
        th_copy(xy.at[left, i], xy.at[left, i], z_s.at[0, i], z_r.at[0, i], left).wait_recv()
        th_copy(xy.at[right, i], xy.at[right, i], z_s.at[1, i], z_r.at[1, i], right).wait_recv()

    def v_copies(i):
        return (
            th_copy(xy.at[left, i, 0], xy.at[left, i, 0], v_s.at[0, i], v_r.at[0, i], right),
            th_copy(xy.at[right, i, 1], xy.at[right, i, 1], v_s.at[1, i], v_r.at[1, i], left),
        )

    def v_wait(i):
        th_copy(xy.at[opp, i, 0], xy.at[opp, i, 0], v_s.at[0, i], v_r.at[0, i], left).wait_recv()
        th_copy(xy.at[opp, i, 1], xy.at[opp, i, 1], v_s.at[1, i], v_r.at[1, i], right).wait_recv()

    def relay(i):
        z_wait(i)
        for copy in v_copies(i):
            copy.start()

    row_own.wait()
    g_own.wait()

    @pl.loop(0, CHUNKS)
    def _(i):
        for part in range(PER):
            base = (i * PER + part) * SET
            for n in range(SET):
                k = base + n

                @pl.when(k > 0)
                def _():
                    row_copy(k).wait_recv()
                    g_copy(k).wait_recv()

            arrived = rr[pl.ds(base, SET)].reshape(SET * SROWS, rr.shape[2])
            wide = rr.shape[2]
            for c in range(4):
                piece = jnp.dot(pack_ref[c], arrived, preferred_element_type=F32).astype(BF16)
                xy[th, i, c // 2, pl.ds(part * SROWS, SROWS), pl.ds(c % 2 * wide, wide)] = piece
        for copy in z_copies(i):
            copy.start()

        @pl.when(i > 0)
        def _():
            relay(i - 1)

    relay(CHUNKS - 1)

    w_own.wait()

    @pl.loop(1, PEERS)
    def _(k):
        w_wait(k)

    quarter = xy.shape[4]
    half = quarter // 2
    blocks = quarter // 128

    def weight(n, first, count):
        return wv[pl.ds(first, count), pl.ds(n * 128, 128), :].reshape(count * 128, cols)

    over_last = (((1,), (1,)), ((), ()))

    def partial(i, j, h):
        da, db = dab[0, i], dab[1, i]
        first = j * blocks + h * (blocks // 2)
        value = lax.dot_general(
            da, weight(0, first, blocks // 2), over_last, preferred_element_type=F32
        ) + lax.dot_general(
            db, weight(1, first, blocks // 2), over_last, preferred_element_type=F32
        )
        return value.astype(BF16)

    row_at = lax.broadcasted_iota(jnp.int32, (SROWS, 128), 0)
    lane_at = lax.broadcasted_iota(jnp.int32, (SROWS, 128), 1)
    source_at = (
        (row_at >= CAP).astype(jnp.int32)
        + (row_at >= 2 * CAP).astype(jnp.int32)
        + (row_at >= 3 * CAP).astype(jnp.int32)
    )
    in_place = lane_at == row_at - source_at * CAP

    def s1_copies(i):
        return (
            th_copy(s1s.at[i, 0], s1r.at[i, 0], s1_s.at[0, i], s1_r.at[0, i], right),
            th_copy(s1s.at[i, 1], s1r.at[i, 1], s1_s.at[1, i], s1_r.at[1, i], left),
        )

    def s2_copies(i):
        return (
            th_copy(s2s.at[i, 0], s2r.at[i, 0], s2_s.at[0, i], s2_r.at[0, i], right),
            th_copy(s2s.at[i, 1], s2r.at[i, 1], s2_s.at[1, i], s2_r.at[1, i], left),
        )

    def b_copy(k):
        return ep_copy(ret.at[k], back_ref.at[k], b_s.at[k], b_r.at[k], peer_from(me, k))

    b_own = pltpu.make_async_copy(ret.at[0], back_ref.at[0], b_r.at[0])

    def combine(i):
        for n, copy in enumerate(s1_copies(i)):
            copy.wait_recv()
            at = pl.ds(n * half, half)
            s2s[i, n, :, at] = (s2s[i, n, :, at].astype(F32) + s1r[i, n].astype(F32)).astype(BF16)
        for copy in s2_copies(i):
            copy.start()

    def finish(i):
        for copy in s2_copies(i):
            copy.wait_recv()
        strip = quarter // 4
        for part in range(PER):
            base = (i * PER + part) * SET
            at = pl.ds(part * SROWS, SROWS)
            packed = jnp.zeros((SET * SROWS, strip), F32)
            for c in range(4):
                span = pl.ds(c * strip, strip)
                total = (
                    own[i, at, span].astype(F32)
                    + s2r[i, 0, at, span].astype(F32)
                    + s2r[i, 1, at, span].astype(F32)
                ).astype(BF16)
                packed += jnp.dot(packt_ref[c], total, preferred_element_type=F32)
            ret[pl.ds(base, SET)] = packed.astype(BF16).reshape(SET, SROWS, strip)
            for n in range(SET):
                k = base + n

                @pl.when(k > 0)
                def _():
                    b_copy(k).start()

                @pl.when(k == 0)
                def _():
                    b_own.start()

    qp[...] = jnp.zeros_like(qp)

    @pl.loop(0, CHUNKS)
    def _(i):
        v_wait(i)
        acc[...] = jnp.zeros_like(acc)

        @pl.loop(0, 4)
        def _(j):
            x, y = xy[j, i, 0], xy[j, i, 1]
            first = j * blocks
            acc[0] += jnp.dot(x, weight(0, first, blocks), preferred_element_type=F32)
            acc[1] += jnp.dot(x, weight(1, first, blocks), preferred_element_type=F32)
            acc[2] += jnp.dot(y, weight(2, first, blocks), preferred_element_type=F32)

        for part in range(PER):
            s = i * PER + part
            at = pl.ds(part * SROWS, SROWS)
            gate = jnp.zeros((SROWS, 128), F32)
            for n in range(SET):
                one = gr[s * SET + n].astype(F32)[0:1, :]
                gate = jnp.where(in_place & (source_at == n), one, gate)
            g = jnp.sum(gate, axis=1, keepdims=True)
            a, b, u = acc[0, at], acc[1, at], acc[2, at]
            sig = jax.nn.sigmoid(a)
            silu = a * sig
            hidden = silu * b
            dh = g * u
            dab[0, i, at] = (dh * b * sig * (1.0 + a * (1.0 - sig))).astype(BF16)
            dab[1, i, at] = (dh * silu).astype(BF16)
            dab[2, i, at] = (g * hidden).astype(BF16)
            q = jnp.sum(u * hidden, axis=1, keepdims=True)
            for n in range(SET):
                mine = jnp.where(in_place & (source_at == n), q, 0.0)
                qp[s, pl.ds(n, 1), :] = jnp.sum(mine, axis=0, keepdims=True)

        s1s[i, 0] = partial(i, opp, 0)
        s1s[i, 1] = partial(i, opp, 1)
        for copy in s1_copies(i):
            copy.start()

        @pl.loop(0, 2)
        def _(h):
            span = pl.ds(pl.multiple_of(h * half, half), half)
            s2s[i, 0, :, span] = partial(i, right, h)
            s2s[i, 1, :, span] = partial(i, left, h)
            own[i, :, span] = partial(i, th, h)

        @pl.when(i > 0)
        def _():
            combine(i - 1)

        @pl.when(i > 1)
        def _():
            finish(i - 2)

    combine(CHUNKS - 1)

    q_copies = tuple(
        th_copy(qp, qr.at[n], q_s.at[n], q_r.at[n], p) for n, p in enumerate((right, left, opp))
    )
    for copy in q_copies:
        copy.start()
    finish(CHUNKS - 2)

    over_rows = (((0,), (0,)), ((), ()))

    def out_copies(t):
        return tuple(
            pltpu.make_async_copy(
                stage.at[t % 2, n], gw_ref.at[n, pl.ds(t * half, half)], o_s.at[t % 2, n]
            )
            for n in range(3)
        )

    def weight_grads(t):
        @pl.when(t > 1)
        def _():
            for copy in out_copies(t - 2):
                copy.wait()

        span = pl.ds(pl.multiple_of(t % 2 * half, half), half)
        for n, kind in enumerate((0, 0, 1)):
            rows = xy[t // 2, :, kind, :, span].reshape(CHUNKS * CROWS, half)
            hid = dab[n].reshape(CHUNKS * CROWS, cols)
            stage[t % 2, n] = lax.dot_general(
                rows, hid, over_rows, preferred_element_type=F32
            ).astype(BF16)
        for copy in out_copies(t):
            copy.start()

    pl.loop(0, 4)(weight_grads)

    finish(CHUNKS - 1)
    for copy in q_copies:
        copy.wait_recv()

    def qb_copy(k):
        return ep_copy(qs.at[k], qback_ref.at[k], qb_s.at[k], qb_r.at[k], peer_from(me, k))

    qb_own = pltpu.make_async_copy(qs.at[0], qback_ref.at[0], qb_r.at[0])
    for s in range(SETS):
        total = qp[s] + qr[0, s] + qr[1, s] + qr[2, s]
        for n in range(SET):
            qs[s * SET + n] = jnp.broadcast_to(total[n : n + 1, :], (16, 128)).astype(BF16)
    qb_own.start()

    @pl.loop(1, PEERS)
    def _(k):
        qb_copy(k).start()

    pl.loop(4, 8)(weight_grads)
    for t in (6, 7):
        for copy in out_copies(t):
            copy.wait()

    qb_own.wait()
    b_own.wait()

    @pl.loop(1, PEERS)
    def _(k):
        row_copy(k).wait_send()
        g_copy(k).wait_send()
        w_copy(k).wait_send()
        b_copy(k).wait()
        qb_copy(k).wait()

    for copy in q_copies:
        copy.wait_send()

    @pl.loop(0, CHUNKS)
    def _(i):
        for copy in (*z_copies(i), *v_copies(i), *s1_copies(i), *s2_copies(i)):
            copy.wait_send()


def layer(rows_send, gate_send, w_send, pack, packt, width, quarter):
    cols = w_send.shape[2]
    wide = rows_send.shape[2]
    strip = quarter // 4
    half = quarter // 2
    dma = pltpu.SemaphoreType.DMA
    peer, ring = dma((PEERS,)), dma((2, CHUNKS))
    anywhere = pl.BlockSpec(memory_space=pl.ANY)
    inside = pl.BlockSpec(memory_space=pltpu.VMEM)
    return pl.pallas_call(
        layer_body,
        out_shape=[
            jax.ShapeDtypeStruct((3, width, cols), BF16),
            jax.ShapeDtypeStruct((PEERS, SROWS, strip), BF16),
            jax.ShapeDtypeStruct((PEERS, 16, 128), BF16),
        ],
        in_specs=[anywhere] * 3 + [inside] * 2,
        out_specs=[anywhere] * 3,
        scratch_shapes=[
            pltpu.VMEM((PEERS, 3 * 128, cols), BF16),
            pltpu.VMEM((4, CHUNKS, 2, CROWS, quarter), BF16),
            pltpu.VMEM((PEERS, SROWS, wide), BF16),
            pltpu.VMEM((PEERS, 16, 128), BF16),
            pltpu.VMEM((3, CHUNKS, CROWS, cols), BF16),
            pltpu.VMEM((3, CROWS, cols), F32),
            pltpu.VMEM((CHUNKS, 2, CROWS, half), BF16),
            pltpu.VMEM((CHUNKS, 2, CROWS, half), BF16),
            pltpu.VMEM((CHUNKS, 2, CROWS, quarter), BF16),
            pltpu.VMEM((CHUNKS, 2, CROWS, quarter), BF16),
            pltpu.VMEM((CHUNKS, CROWS, quarter), BF16),
            pltpu.VMEM((PEERS, SROWS, strip), BF16),
            pltpu.VMEM((SETS, 8, 128), F32),
            pltpu.VMEM((3, SETS, 8, 128), F32),
            pltpu.VMEM((PEERS, 16, 128), BF16),
            pltpu.VMEM((2, 3, half, cols), BF16),
            peer, peer, peer, peer, peer, peer,
            ring, ring, ring, ring, ring, ring, ring, ring,
            peer, peer, dma((3,)), dma((3,)), peer, peer, dma((2, 3)),
        ],
        compiler_params=pltpu.CompilerParams(
            collective_id=0, has_side_effects=True, vmem_limit_bytes=63 * 2**20
        ),
    )(rows_send, gate_send, w_send, pack, packt)


def local(tokens, cotangent, gates, routing, new_slot, gate_old, up_old, down_old):
    tok_count = routing.shape[0]
    quarter = tokens.shape[1]
    ids = jnp.arange(PEERS, dtype=jnp.int32)
    expert = peer_to(lax.axis_index("ep"), ids)
    order = jnp.sum(
        (new_slot[None, :] == expert[:, None]).astype(jnp.int32) * ids[None, :], axis=1
    )
    w_send = reorder(order, gate_old, up_old, down_old)
    named = routing[:, :, None] == expert[None, None, :]
    hits = jnp.any(named, axis=1)
    at = jnp.arange(tok_count, dtype=jnp.int32)
    below = (at[:, None] > at[None, :]).astype(BF16)
    rank = jnp.dot(below, hits.astype(BF16), preferred_element_type=F32)
    place = jnp.where(hits, rank, -1.0).astype(jnp.int32)
    ranks = jnp.arange(CAP, dtype=jnp.int32)
    pick = place.T[:, None, :] == ranks[None, :, None]
    group = jnp.arange(4, dtype=jnp.int32)
    spread = (
        pick[:, None, :, None, :] & (group[:, None] == group[None, :])[None, :, None, :, None]
    ).astype(BF16)
    spread = spread.reshape(PEERS * 4 * CAP, 4 * tok_count)
    both = jnp.concatenate([tokens, cotangent], axis=1)
    stacked = both.reshape(tok_count, 4, -1).transpose(1, 0, 2).reshape(4 * tok_count, -1)
    rows_send = jnp.dot(spread, stacked, preferred_element_type=F32).astype(BF16)
    gate_of = jnp.sum(jnp.where(named, gates.astype(F32)[:, :, None], 0.0), axis=1)
    gate_rows = jnp.sum(jnp.where(pick, gate_of.T[:, None, :], 0.0), axis=2)
    gate_send = jnp.broadcast_to(
        jnp.pad(gate_rows, ((0, 0), (0, 128 - CAP)))[:, None, :], (PEERS, 16, 128)
    ).astype(BF16)
    row = jnp.arange(SROWS, dtype=jnp.int32)
    from_row = (row // CAP * SROWS + row % CAP)[None, :] + group[:, None] * CAP
    spot = jnp.arange(SET * SROWS, dtype=jnp.int32)
    pack = (from_row[:, :, None] == spot[None, None, :]).astype(BF16)
    packt = (from_row[:, None, :] == spot[None, :, None]).astype(BF16)
    width = quarter * lax.axis_size("th")
    grads, back, qback = layer(
        rows_send.reshape(PEERS, SROWS, -1), gate_send, w_send, pack, packt, width, quarter
    )
    grad_stack = lax.dot_general(
        spread,
        back.reshape(PEERS * SROWS, -1),
        (((0,), (0,)), ((), ())),
        preferred_element_type=F32,
    ).astype(BF16)
    grad_tokens = (
        grad_stack.reshape(4, tok_count, -1).transpose(1, 0, 2).reshape(tok_count, quarter)
    )
    router = qback[:, 0, :CAP].astype(F32)
    router_of = jnp.sum(jnp.where(pick, router[:, :, None], 0.0), axis=1).T
    grad_gates = jnp.sum(jnp.where(named, router_of[:, None, :], 0.0), axis=2)
    return (grad_tokens, grad_gates.astype(BF16), grads[0:1], grads[1:2], grads[2:3])


def solution(mesh):
    placed = (
        P("ep", "th"),
        P("ep", "th"),
        P("ep", None),
        P("ep", None),
        P(),
        P(None, "ep", "th"),
        P(None, "ep", "th"),
        P(None, "ep", "th"),
    )
    return jax.shard_map(
        local,
        mesh=mesh,
        in_specs=placed,
        out_specs=(
            P("ep", "th"),
            P("ep", None),
            P("ep", None, "th"),
            P("ep", None, "th"),
            P("ep", None, "th"),
        ),
        check_vma=False,
    )
```

```python
import jax
import jax.numpy as jnp
from jax import lax
from jax.experimental import pallas as pl
from jax.experimental.pallas import tpu as pltpu
from jax.sharding import PartitionSpec as P

CAP = 36
PEERS = 32
SET = 4
CHUNKS = 4
SETS = PEERS // SET
PER = SETS // CHUNKS
SROWS = SET * CAP
CROWS = PER * SROWS
MESH = pl.DeviceIdType.MESH
F32 = jnp.float32
BF16 = jnp.bfloat16


def offset(core, k):
    m, sign = k % 16, 1 + 2 * core
    return m % 4 * sign % 4, (m // 4 + m % 4) % 4 * sign % 4, k // 16


def peer_to(me, k):
    dx, dy, dc = offset(me % 2, k)
    return (me // 8 + dx) % 4 * 8 + ((me // 2) % 4 + dy) % 4 * 2 + (me % 2 + dc) % 2


def peer_from(me, k):
    core = (me % 2 + k // 16) % 2
    dx, dy, _ = offset(core, k)
    return (me // 8 + 4 - dx) % 4 * 8 + ((me // 2) % 4 + 4 - dy) % 4 * 2 + core


def reorder_body(order, gate_ref, up_ref, down_ref, out_ref, held, in_sems, out_sems):
    depth = gate_ref.shape[1]

    def reads(k):
        return [
            pltpu.make_async_copy(
                ref.at[order[k]], held.at[k, pl.ds(n * depth, depth)], in_sems.at[n, k]
            )
            for n, ref in enumerate((gate_ref, up_ref, down_ref))
        ]

    def write(k):
        return pltpu.make_async_copy(held.at[k], out_ref.at[k], out_sems.at[k])

    @pl.loop(0, PEERS, unroll=8)
    def _(k):
        for copy in reads(k):
            copy.start()

    @pl.loop(0, PEERS)
    def _(k):
        for copy in reads(k):
            copy.wait()
        write(k).start()

    @pl.loop(0, PEERS)
    def _(k):
        write(k).wait()


def reorder(order, gate_old, up_old, down_old):
    count, depth, cols = gate_old.shape
    return pl.pallas_call(
        reorder_body,
        out_shape=jax.ShapeDtypeStruct((count, 3 * depth, cols), gate_old.dtype),
        grid_spec=pltpu.PrefetchScalarGridSpec(
            num_scalar_prefetch=1,
            grid=(),
            in_specs=[pl.BlockSpec(memory_space=pl.ANY)] * 3,
            out_specs=pl.BlockSpec(memory_space=pl.ANY),
            scratch_shapes=[
                pltpu.VMEM((count, 3 * depth, cols), gate_old.dtype),
                pltpu.SemaphoreType.DMA((3, count)),
                pltpu.SemaphoreType.DMA((count,)),
            ],
        ),
        compiler_params=pltpu.CompilerParams(vmem_limit_bytes=24 * 2**20),
    )(order, gate_old, up_old, down_old)


def layer_body(
    rows_ref, gsend_ref, wsend_ref, pack_ref, packt_ref,
    gw_ref, back_ref, qback_ref,
    wv, xy, rr, gr, dab, acc, s1s, s1r, s2s, s2r, own, ret, qp, qr, qs, stage,
    row_s, row_r, g_s, g_r, w_s, w_r, z_s, z_r, v_s, v_r, s1_s, s1_r, s2_s, s2_r, d_s, d_r,
    b_s, b_r, q_s, q_r, qb_s, qb_r, o_s,
):
    me = lax.axis_index("ep")
    th = lax.axis_index("th")
    right, left, opp = (th + 1) % 4, (th + 3) % 4, (th + 2) % 4
    cols = wv.shape[2]

    def ep_copy(src, dst, s, r, p):
        return pltpu.make_async_remote_copy(
            src_ref=src, dst_ref=dst, send_sem=s, recv_sem=r, device_id={"ep": p},
            device_id_type=MESH,
        )

    def th_copy(src, dst, s, r, p):
        return pltpu.make_async_remote_copy(
            src_ref=src, dst_ref=dst, send_sem=s, recv_sem=r, device_id={"th": p},
            device_id_type=MESH,
        )

    barrier = pltpu.get_barrier_semaphore()

    @pl.loop(1, PEERS)
    def _(k):
        pl.semaphore_signal(
            barrier, inc=1, device_id={"ep": peer_to(me, k)}, device_id_type=MESH
        )

    for p in (right, left, opp):
        pl.semaphore_signal(barrier, inc=1, device_id={"th": p}, device_id_type=MESH)
    pl.semaphore_wait(barrier, PEERS - 1 + 3)

    def row_copy(k):
        return ep_copy(rows_ref.at[k], rr.at[k], row_s.at[k], row_r.at[k], peer_to(me, k))

    def g_copy(k):
        return ep_copy(gsend_ref.at[k], gr.at[k], g_s.at[k], g_r.at[k], peer_to(me, k))

    def w_copy(k):
        return ep_copy(wsend_ref.at[k], wv.at[me], w_s.at[k], w_r.at[k], peer_to(me, k))

    def w_wait(k):
        s = peer_from(me, k)
        ep_copy(wsend_ref.at[k], wv.at[s], w_s.at[k], w_r.at[k], s).wait_recv()

    row_own = pltpu.make_async_copy(rows_ref.at[0], rr.at[0], row_r.at[0])
    g_own = pltpu.make_async_copy(gsend_ref.at[0], gr.at[0], g_r.at[0])
    w_own = pltpu.make_async_copy(wsend_ref.at[0], wv.at[me], w_r.at[0])
    row_own.start()
    g_own.start()

    def send_rows(first, last):
        @pl.loop(first, last)
        def _(k):
            g_copy(k).start()
            row_copy(k).start()

    send_rows(1, 3 * SET)
    w_own.start()

    def z_copies(i):
        return (
            th_copy(xy.at[th, i], xy.at[th, i], z_s.at[0, i], z_r.at[0, i], right),
            th_copy(xy.at[th, i], xy.at[th, i], z_s.at[1, i], z_r.at[1, i], left),
        )

    def z_wait(i):
        th_copy(xy.at[left, i], xy.at[left, i], z_s.at[0, i], z_r.at[0, i], left).wait_recv()
        th_copy(xy.at[right, i], xy.at[right, i], z_s.at[1, i], z_r.at[1, i], right).wait_recv()

    def v_copies(i):
        return (
            th_copy(xy.at[left, i, 0], xy.at[left, i, 0], v_s.at[0, i], v_r.at[0, i], right),
            th_copy(xy.at[right, i, 1], xy.at[right, i, 1], v_s.at[1, i], v_r.at[1, i], left),
        )

    def v_wait(i):
        th_copy(xy.at[opp, i, 0], xy.at[opp, i, 0], v_s.at[0, i], v_r.at[0, i], left).wait_recv()
        th_copy(xy.at[opp, i, 1], xy.at[opp, i, 1], v_s.at[1, i], v_r.at[1, i], right).wait_recv()

    def relay(i):
        z_wait(i)
        for copy in v_copies(i):
            copy.start()

    row_own.wait()
    g_own.wait()

    @pl.loop(0, SETS)
    def _(i):
        for n in range(SET):
            k = i * SET + n

            @pl.when(k > 0)
            def _():
                row_copy(k).wait_recv()
                g_copy(k).wait_recv()

        @pl.when(i == 0)
        def _():
            send_rows(3 * SET, 6 * SET)

        arrived = rr[pl.ds(i * SET, SET)].reshape(SET * SROWS, rr.shape[2])
        wide = rr.shape[2]
        for c in range(4):
            piece = jnp.dot(pack_ref[c], arrived, preferred_element_type=F32).astype(BF16)
            xy[th, i, c // 2, :, pl.ds(c % 2 * wide, wide)] = piece
        for copy in z_copies(i):
            copy.start()

        @pl.when(i == 1)
        def _():
            send_rows(6 * SET, PEERS)

            @pl.loop(1, PEERS)
            def _(k):
                w_copy(k).start()

        @pl.when(i > 0)
        def _():
            relay(i - 1)

    relay(SETS - 1)

    w_own.wait()

    @pl.loop(1, PEERS)
    def _(k):
        w_wait(k)

    quarter = xy.shape[4]
    half = quarter // 2
    blocks = quarter // 128

    def weight(n, first, count):
        return wv[pl.ds(first, count), pl.ds(n * 128, 128), :].reshape(count * 128, cols)

    over_last = (((1,), (1,)), ((), ()))

    def partial(i, j, h):
        da, db = dab[0, i], dab[1, i]
        first = j * blocks + h * (blocks // 2)
        value = lax.dot_general(
            da, weight(0, first, blocks // 2), over_last, preferred_element_type=F32
        ) + lax.dot_general(
            db, weight(1, first, blocks // 2), over_last, preferred_element_type=F32
        )
        return value.astype(BF16)

    row_at = lax.broadcasted_iota(jnp.int32, (SROWS, 128), 0)
    lane_at = lax.broadcasted_iota(jnp.int32, (SROWS, 128), 1)
    source_at = (
        (row_at >= CAP).astype(jnp.int32)
        + (row_at >= 2 * CAP).astype(jnp.int32)
        + (row_at >= 3 * CAP).astype(jnp.int32)
    )
    in_place = lane_at == row_at - source_at * CAP

    def s1_copies(i):
        return (
            th_copy(s1s.at[i, 0], s1r.at[i, 0], s1_s.at[0, i], s1_r.at[0, i], right),
            th_copy(s1s.at[i, 1], s1r.at[i, 1], s1_s.at[1, i], s1_r.at[1, i], left),
        )

    def s2_copies(i):
        return (
            th_copy(s2s.at[i, 0, 0], s2r.at[i, 0, 0], s2_s.at[0, i], s2_r.at[0, i], right),
            th_copy(s2s.at[i, 1, 1], s2r.at[i, 1, 1], s2_s.at[1, i], s2_r.at[1, i], left),
        )

    def d_copies(i):
        return (
            th_copy(s2s.at[i, 0, 1], s2r.at[i, 0, 1], d_s.at[0, i], d_r.at[0, i], right),
            th_copy(s2s.at[i, 1, 0], s2r.at[i, 1, 0], d_s.at[1, i], d_r.at[1, i], left),
        )

    def b_copy(k):
        return ep_copy(ret.at[k], back_ref.at[k], b_s.at[k], b_r.at[k], peer_from(me, k))

    b_own = pltpu.make_async_copy(ret.at[0], back_ref.at[0], b_r.at[0])

    def combine(i):
        for n, copy in enumerate(s1_copies(i)):
            copy.wait_recv()
            s2s[i, n, n] = (s2s[i, n, n].astype(F32) + s1r[i, n].astype(F32)).astype(BF16)
        for copy in s2_copies(i):
            copy.start()

    def finish(i):
        for copy in (*d_copies(i), *s2_copies(i)):
            copy.wait_recv()
        strip = quarter // 4
        for part in range(PER):
            base = (i * PER + part) * SET
            at = pl.ds(part * SROWS, SROWS)
            packed = jnp.zeros((SET * SROWS, strip), F32)
            for c in range(4):
                h, span = c // 2, pl.ds(c % 2 * strip, strip)
                total = (
                    own[i, h, at, span].astype(F32)
                    + s2r[i, 0, h, at, span].astype(F32)
                    + s2r[i, 1, h, at, span].astype(F32)
                ).astype(BF16)
                packed += jnp.dot(packt_ref[c], total, preferred_element_type=F32)
            ret[pl.ds(base, SET)] = packed.astype(BF16).reshape(SET, SROWS, strip)
            for n in range(SET):
                k = base + n

                @pl.when(k > 0)
                def _():
                    b_copy(k).start()

                @pl.when(k == 0)
                def _():
                    b_own.start()

    qp[...] = jnp.zeros_like(qp)

    @pl.loop(0, CHUNKS)
    def _(i):
        for part in range(PER):
            v_wait(i * PER + part)
        acc[...] = jnp.zeros_like(acc)

        @pl.loop(0, 4)
        def _(j):
            x = xy[j, pl.ds(i * PER, PER), 0].reshape(CROWS, quarter)
            y = xy[j, pl.ds(i * PER, PER), 1].reshape(CROWS, quarter)
            first = j * blocks
            acc[0] += jnp.dot(x, weight(0, first, blocks), preferred_element_type=F32)
            acc[1] += jnp.dot(x, weight(1, first, blocks), preferred_element_type=F32)
            acc[2] += jnp.dot(y, weight(2, first, blocks), preferred_element_type=F32)

        for part in range(PER):
            s = i * PER + part
            at = pl.ds(part * SROWS, SROWS)
            gate = jnp.zeros((SROWS, 128), F32)
            for n in range(SET):
                one = gr[s * SET + n].astype(F32)[0:1, :]
                gate = jnp.where(in_place & (source_at == n), one, gate)
            g = jnp.sum(gate, axis=1, keepdims=True)
            a, b, u = acc[0, at], acc[1, at], acc[2, at]
            sig = jax.nn.sigmoid(a)
            silu = a * sig
            hidden = silu * b
            dh = g * u
            dab[0, i, at] = (dh * b * sig * (1.0 + a * (1.0 - sig))).astype(BF16)
            dab[1, i, at] = (dh * silu).astype(BF16)
            dab[2, i, at] = (g * hidden).astype(BF16)
            q = jnp.sum(u * hidden, axis=1, keepdims=True)
            for n in range(SET):
                mine = jnp.where(in_place & (source_at == n), q, 0.0)
                qp[s, pl.ds(n, 1), :] = jnp.sum(mine, axis=0, keepdims=True)

        s1s[i, 0] = partial(i, opp, 0)
        s1s[i, 1] = partial(i, opp, 1)
        for copy in s1_copies(i):
            copy.start()

        @pl.loop(0, 2)
        def _(h):
            s2s[i, 0, 1 - h] = partial(i, right, 1 - h)
            s2s[i, 1, h] = partial(i, left, h)

            @pl.when(h == 0)
            def _():
                for copy in d_copies(i):
                    copy.start()

            own[i, h] = partial(i, th, h)

        @pl.when(i > 0)
        def _():
            combine(i - 1)

        @pl.when(i > 1)
        def _():
            finish(i - 2)

    combine(CHUNKS - 1)

    q_copies = tuple(
        th_copy(qp, qr.at[n], q_s.at[n], q_r.at[n], p) for n, p in enumerate((right, left, opp))
    )
    for copy in q_copies:
        copy.start()
    finish(CHUNKS - 2)

    over_rows = (((0,), (0,)), ((), ()))

    def out_copies(t):
        return tuple(
            pltpu.make_async_copy(
                stage.at[t % 2, n], gw_ref.at[n, pl.ds(t * half, half)], o_s.at[t % 2, n]
            )
            for n in range(3)
        )

    def weight_grads(t):
        @pl.when(t > 1)
        def _():
            for copy in out_copies(t - 2):
                copy.wait()

        span = pl.ds(pl.multiple_of(t % 2 * half, half), half)
        for n, kind in enumerate((0, 0, 1)):
            rows = xy[t // 2, :, kind, :, span].reshape(SETS * SROWS, half)
            hid = dab[n].reshape(CHUNKS * CROWS, cols)
            stage[t % 2, n] = lax.dot_general(
                rows, hid, over_rows, preferred_element_type=F32
            ).astype(BF16)
        for copy in out_copies(t):
            copy.start()

    pl.loop(0, 4)(weight_grads)

    finish(CHUNKS - 1)
    for copy in q_copies:
        copy.wait_recv()

    def qb_copy(k):
        return ep_copy(qs.at[k], qback_ref.at[k], qb_s.at[k], qb_r.at[k], peer_from(me, k))

    qb_own = pltpu.make_async_copy(qs.at[0], qback_ref.at[0], qb_r.at[0])
    for s in range(SETS):
        total = qp[s] + qr[0, s] + qr[1, s] + qr[2, s]
        for n in range(SET):
            qs[s * SET + n] = jnp.broadcast_to(total[n : n + 1, :], (16, 128)).astype(BF16)
    qb_own.start()

    @pl.loop(1, PEERS)
    def _(k):
        qb_copy(k).start()

    pl.loop(4, 8)(weight_grads)
    for t in (6, 7):
        for copy in out_copies(t):
            copy.wait()

    qb_own.wait()
    b_own.wait()

    @pl.loop(1, PEERS)
    def _(k):
        row_copy(k).wait_send()
        g_copy(k).wait_send()
        w_copy(k).wait_send()
        b_copy(k).wait()
        qb_copy(k).wait()

    for copy in q_copies:
        copy.wait_send()

    @pl.loop(0, SETS)
    def _(i):
        for copy in (*z_copies(i), *v_copies(i)):
            copy.wait_send()

    @pl.loop(0, CHUNKS)
    def _(i):
        for copy in (*s1_copies(i), *d_copies(i), *s2_copies(i)):
            copy.wait_send()


def layer(rows_send, gate_send, w_send, pack, packt, width, quarter):
    cols = w_send.shape[2]
    wide = rows_send.shape[2]
    strip = quarter // 4
    half = quarter // 2
    dma = pltpu.SemaphoreType.DMA
    peer, sets, ring = dma((PEERS,)), dma((2, SETS)), dma((2, CHUNKS))
    anywhere = pl.BlockSpec(memory_space=pl.ANY)
    inside = pl.BlockSpec(memory_space=pltpu.VMEM)
    return pl.pallas_call(
        layer_body,
        out_shape=[
            jax.ShapeDtypeStruct((3, width, cols), BF16),
            jax.ShapeDtypeStruct((PEERS, SROWS, strip), BF16),
            jax.ShapeDtypeStruct((PEERS, 16, 128), BF16),
        ],
        in_specs=[anywhere] * 3 + [inside] * 2,
        out_specs=[anywhere] * 3,
        scratch_shapes=[
            pltpu.VMEM((PEERS, 3 * 128, cols), BF16),
            pltpu.VMEM((4, SETS, 2, SROWS, quarter), BF16),
            pltpu.VMEM((PEERS, SROWS, wide), BF16),
            pltpu.VMEM((PEERS, 16, 128), BF16),
            pltpu.VMEM((3, CHUNKS, CROWS, cols), BF16),
            pltpu.VMEM((3, CROWS, cols), F32),
            pltpu.VMEM((CHUNKS, 2, CROWS, half), BF16),
            pltpu.VMEM((CHUNKS, 2, CROWS, half), BF16),
            pltpu.VMEM((CHUNKS, 2, 2, CROWS, half), BF16),
            pltpu.VMEM((CHUNKS, 2, 2, CROWS, half), BF16),
            pltpu.VMEM((CHUNKS, 2, CROWS, half), BF16),
            pltpu.VMEM((PEERS, SROWS, strip), BF16),
            pltpu.VMEM((SETS, 8, 128), F32),
            pltpu.VMEM((3, SETS, 8, 128), F32),
            pltpu.VMEM((PEERS, 16, 128), BF16),
            pltpu.VMEM((2, 3, half, cols), BF16),
            peer, peer, peer, peer, peer, peer,
            sets, sets, sets, sets, ring, ring, ring, ring, ring, ring,
            peer, peer, dma((3,)), dma((3,)), peer, peer, dma((2, 3)),
        ],
        compiler_params=pltpu.CompilerParams(
            collective_id=0, has_side_effects=True, vmem_limit_bytes=63 * 2**20
        ),
    )(rows_send, gate_send, w_send, pack, packt)


def local(tokens, cotangent, gates, routing, new_slot, gate_old, up_old, down_old):
    tok_count = routing.shape[0]
    quarter = tokens.shape[1]
    ids = jnp.arange(PEERS, dtype=jnp.int32)
    expert = peer_to(lax.axis_index("ep"), ids)
    order = jnp.sum(
        (new_slot[None, :] == expert[:, None]).astype(jnp.int32) * ids[None, :], axis=1
    )
    w_send = reorder(order, gate_old, up_old, down_old)
    named = routing[:, :, None] == expert[None, None, :]
    hits = jnp.any(named, axis=1)
    at = jnp.arange(tok_count, dtype=jnp.int32)
    below = (at[:, None] > at[None, :]).astype(BF16)
    rank = jnp.dot(below, hits.astype(BF16), preferred_element_type=F32)
    place = jnp.where(hits, rank, -1.0).astype(jnp.int32)
    ranks = jnp.arange(CAP, dtype=jnp.int32)
    pick = place.T[:, None, :] == ranks[None, :, None]
    group = jnp.arange(4, dtype=jnp.int32)
    spread = (
        pick[:, None, :, None, :] & (group[:, None] == group[None, :])[None, :, None, :, None]
    ).astype(BF16)
    spread = spread.reshape(PEERS * 4 * CAP, 4 * tok_count)
    both = jnp.concatenate([tokens, cotangent], axis=1)
    stacked = both.reshape(tok_count, 4, -1).transpose(1, 0, 2).reshape(4 * tok_count, -1)
    rows_send = jnp.dot(spread, stacked, preferred_element_type=F32).astype(BF16)
    gate_of = jnp.sum(jnp.where(named, gates.astype(F32)[:, :, None], 0.0), axis=1)
    gate_rows = jnp.sum(jnp.where(pick, gate_of.T[:, None, :], 0.0), axis=2)
    gate_send = jnp.broadcast_to(
        jnp.pad(gate_rows, ((0, 0), (0, 128 - CAP)))[:, None, :], (PEERS, 16, 128)
    ).astype(BF16)
    row = jnp.arange(SROWS, dtype=jnp.int32)
    from_row = (row // CAP * SROWS + row % CAP)[None, :] + group[:, None] * CAP
    spot = jnp.arange(SET * SROWS, dtype=jnp.int32)
    pack = (from_row[:, :, None] == spot[None, None, :]).astype(BF16)
    packt = (from_row[:, None, :] == spot[None, :, None]).astype(BF16)
    width = quarter * lax.axis_size("th")
    grads, back, qback = layer(
        rows_send.reshape(PEERS, SROWS, -1), gate_send, w_send, pack, packt, width, quarter
    )
    grad_stack = lax.dot_general(
        spread,
        back.reshape(PEERS * SROWS, -1),
        (((0,), (0,)), ((), ())),
        preferred_element_type=F32,
    ).astype(BF16)
    grad_tokens = (
        grad_stack.reshape(4, tok_count, -1).transpose(1, 0, 2).reshape(tok_count, quarter)
    )
    router = qback[:, 0, :CAP].astype(F32)
    router_of = jnp.sum(jnp.where(pick, router[:, :, None], 0.0), axis=1).T
    grad_gates = jnp.sum(jnp.where(named, router_of[:, None, :], 0.0), axis=2)
    return (grad_tokens, grad_gates.astype(BF16), grads[0:1], grads[1:2], grads[2:3])


def solution(mesh):
    placed = (
        P("ep", "th"),
        P("ep", "th"),
        P("ep", None),
        P("ep", None),
        P(),
        P(None, "ep", "th"),
        P(None, "ep", "th"),
        P(None, "ep", "th"),
    )
    return jax.shard_map(
        local,
        mesh=mesh,
        in_specs=placed,
        out_specs=(
            P("ep", "th"),
            P("ep", None),
            P("ep", None, "th"),
            P("ep", None, "th"),
            P("ep", None, "th"),
        ),
        check_vma=False,
    )
```

```python
import jax
import jax.numpy as jnp
from jax import lax
from jax.experimental import pallas as pl
from jax.experimental.pallas import tpu as pltpu
from jax.sharding import PartitionSpec as P

CAP = 36
PEERS = 32
SET = 4
CHUNKS = 4
SETS = PEERS // SET
PER = SETS // CHUNKS
SROWS = SET * CAP
CROWS = PER * SROWS
MESH = pl.DeviceIdType.MESH
F32 = jnp.float32
BF16 = jnp.bfloat16


def offset(core, k):
    m, sign = k % 16, 1 + 2 * core
    return m % 4 * sign % 4, (m // 4 + m % 4) % 4 * sign % 4, k // 16


def peer_to(me, k):
    dx, dy, dc = offset(me % 2, k)
    return (me // 8 + dx) % 4 * 8 + ((me // 2) % 4 + dy) % 4 * 2 + (me % 2 + dc) % 2


def peer_from(me, k):
    core = (me % 2 + k // 16) % 2
    dx, dy, _ = offset(core, k)
    return (me // 8 + 4 - dx) % 4 * 8 + ((me // 2) % 4 + 4 - dy) % 4 * 2 + core


def layer_body(
    order_ref, tokens_ref, cot_ref, gates_ref, routing_ref, expert_ref, gate_ref, up_ref, down_ref,
    gw_ref, back_ref, tok_out, gates_out,
    wv, xy, rr, gr, gs, acc, s1s, s1r, s2s, s2r, own, qp, qr, qb, pool, bounce, pack,
    spots, shares, routed,
    row_s, row_r, g_s, g_r, w_s, w_r, z_s, z_r, v_s, v_r, s1_s, s1_r, s2_s, s2_r, d_s, d_r,
    b_s, b_r, q_s, q_r, qb_s, qb_r, o_s, p_s, l_s,
):
    me = lax.axis_index("ep")
    th = lax.axis_index("th")
    right, left, opp = (th + 1) % 4, (th + 3) % 4, (th + 2) % 4
    cols = wv.shape[2]
    over_last = (((1,), (1,)), ((), ()))
    over_rows = (((0,), (0,)), ((), ()))

    def ep_copy(src, dst, s, r, p):
        return pltpu.make_async_remote_copy(
            src_ref=src, dst_ref=dst, send_sem=s, recv_sem=r, device_id={"ep": p},
            device_id_type=MESH,
        )

    def th_copy(src, dst, s, r, p):
        return pltpu.make_async_remote_copy(
            src_ref=src, dst_ref=dst, send_sem=s, recv_sem=r, device_id={"th": p},
            device_id_type=MESH,
        )

    barrier = pltpu.get_barrier_semaphore()

    @pl.loop(1, PEERS)
    def _(k):
        pl.semaphore_signal(
            barrier, inc=1, device_id={"ep": peer_to(me, k)}, device_id_type=MESH
        )

    for p in (right, left, opp):
        pl.semaphore_signal(barrier, inc=1, device_id={"th": p}, device_id_type=MESH)
    def pool_copy(n):
        return pltpu.make_async_copy((gate_ref, up_ref, down_ref)[n], pool.at[:, pl.ds(0, 128)], p_s.at[n])

    pool_copy(0).start()

    tok_count = tokens_ref.shape[0]
    quarter = tokens_ref.shape[1]
    half = quarter // 2
    strip = quarter // 4
    pair = 2 * tok_count
    top_count = routing_ref.shape[0]
    expert = expert_ref[...]
    hits = jnp.zeros((PEERS, tok_count), F32)
    share = jnp.zeros((PEERS, tok_count), F32)
    for n in range(top_count):
        same = routing_ref[pl.ds(n, 1), :] == expert
        hits = jnp.where(same, 1.0, hits)
        share = jnp.where(same, gates_ref[pl.ds(n, 1), :], share)
    earlier = lax.broadcasted_iota(jnp.int32, (tok_count, tok_count), 0) < (
        lax.broadcasted_iota(jnp.int32, (tok_count, tok_count), 1)
    )
    rank = jnp.dot(hits.astype(BF16), earlier.astype(F32).astype(BF16), preferred_element_type=F32)
    for c in range(4):
        spot = jnp.where(hits > 0.5, rank + float(c * CAP), -1.0)
        spots[:, pl.ds(c * tok_count, tok_count)] = spot
    shares[...] = share
    for c in range(2):
        at = pl.ds(c * half, half)
        own[0, 0, pl.ds(c * tok_count, tok_count), :] = tokens_ref[:, at]
        own[0, 1, pl.ds(c * tok_count, tok_count), :] = cot_ref[:, at]
    wide_row = lax.broadcasted_iota(jnp.int32, (SROWS, SET * SROWS), 0)
    wide_spot = lax.broadcasted_iota(jnp.int32, (SROWS, SET * SROWS), 1)
    for m in range(1, SET):
        wide_spot = wide_spot - jnp.where(wide_row >= m * CAP, SROWS - CAP, 0)
    for c in range(4):
        pack[c] = (wide_spot == wide_row + c * CAP).astype(F32).astype(BF16)
    row_ids = lax.broadcasted_iota(jnp.int32, (SROWS, 4 * tok_count), 0).astype(F32)

    def one_hot(k):
        return (row_ids == spots[pl.ds(k, 1), :]).astype(F32).astype(BF16)

    pl.semaphore_wait(barrier, PEERS - 1 + 3)

    def row_slot(k):
        return s2s.at[k // 8, k // 4 % 2, k // 2 % 2, pl.ds(k % 2 * SROWS, SROWS)]

    def row_copy(k):
        return ep_copy(row_slot(k), rr.at[k], row_s.at[k], row_r.at[k], peer_to(me, k))

    def g_copy(k):
        return ep_copy(gs.at[k], gr.at[k], g_s.at[k], g_r.at[k], peer_to(me, k))

    def build(k):
        chosen = one_hot(k)
        block = jnp.dot(chosen[:, :pair], own[0, 0, :pair, :], preferred_element_type=F32)
        block = block + jnp.dot(chosen[:, pair:], own[0, 1, :pair, :], preferred_element_type=F32)
        s2s[k // 8, k // 4 % 2, k // 2 % 2, pl.ds(pl.multiple_of(k % 2 * SROWS, 16), SROWS)] = (
            block.astype(BF16)
        )
        mine = jnp.broadcast_to(shares[pl.ds(k, 1), :], (16, tok_count)).astype(BF16)
        gs[k] = lax.dot_general(
            mine, chosen[:128, :tok_count], over_last, preferred_element_type=F32
        ).astype(BF16)

    def w_copy(n, k):
        return ep_copy(
            bounce.at[n % 2, k], wv.at[me, pl.ds(n * 128, 128)], w_s.at[n, k], w_r.at[n, k],
            peer_to(me, k),
        )

    def w_wait(n, k):
        s = peer_from(me, k)
        ep_copy(
            bounce.at[n % 2, k], wv.at[s, pl.ds(n * 128, 128)], w_s.at[n, k], w_r.at[n, k], s
        ).wait_recv()

    def w_own(n):
        return pltpu.make_async_copy(
            bounce.at[n % 2, 0], wv.at[me, pl.ds(n * 128, 128)], w_r.at[n, 0]
        )

    def send_weights(n):
        pool_copy(n).wait()

        @pl.loop(0, PEERS)
        def _(k):
            bounce[n % 2, k] = pool[order_ref[k]][:128]

            @pl.when(k > 0)
            def _():
                w_copy(n, k).start()

        w_own(n).start()
        if n < 2:
            pool_copy(n + 1).start()

    def wait_weights(n):
        w_own(n).wait()

        @pl.loop(1, PEERS)
        def _(k):
            w_copy(n, k).wait_send()

    row_own = pltpu.make_async_copy(row_slot(0), rr.at[0], row_r.at[0])
    g_own = pltpu.make_async_copy(gs.at[0], gr.at[0], g_r.at[0])

    def send_rows(first, last):
        @pl.loop(first, last)
        def _(k):
            build(k)
            g_copy(k).start()
            row_copy(k).start()

    build(0)
    row_own.start()
    g_own.start()
    send_rows(1, 3 * SET)

    def z_copies(i):
        return (
            th_copy(xy.at[th, i], xy.at[th, i], z_s.at[0, i], z_r.at[0, i], right),
            th_copy(xy.at[th, i], xy.at[th, i], z_s.at[1, i], z_r.at[1, i], left),
        )

    def z_wait(i):
        th_copy(xy.at[left, i], xy.at[left, i], z_s.at[0, i], z_r.at[0, i], left).wait_recv()
        th_copy(xy.at[right, i], xy.at[right, i], z_s.at[1, i], z_r.at[1, i], right).wait_recv()

    def v_copies(i):
        return (
            th_copy(xy.at[left, i, 0], xy.at[left, i, 0], v_s.at[0, i], v_r.at[0, i], right),
            th_copy(xy.at[right, i, 1], xy.at[right, i, 1], v_s.at[1, i], v_r.at[1, i], left),
        )

    def v_wait(i):
        th_copy(xy.at[opp, i, 0], xy.at[opp, i, 0], v_s.at[0, i], v_r.at[0, i], left).wait_recv()
        th_copy(xy.at[opp, i, 1], xy.at[opp, i, 1], v_s.at[1, i], v_r.at[1, i], right).wait_recv()

    def relay(i):
        z_wait(i)
        for copy in v_copies(i):
            copy.start()

    row_own.wait()
    g_own.wait()

    @pl.loop(0, SETS)
    def _(i):
        for n in range(SET):
            k = i * SET + n

            @pl.when(k > 0)
            def _():
                row_copy(k).wait_recv()
                g_copy(k).wait_recv()

        @pl.when(i == 0)
        def _():
            send_rows(3 * SET, 6 * SET)

        arrived = rr[pl.ds(i * SET, SET)].reshape(SET * SROWS, rr.shape[2])
        wide = rr.shape[2]
        for c in range(4):
            piece = jnp.dot(pack[c], arrived, preferred_element_type=F32).astype(BF16)
            xy[th, i, c // 2, :, pl.ds(c % 2 * wide, wide)] = piece
        for copy in z_copies(i):
            copy.start()

        @pl.when(i == 1)
        def _():
            send_rows(6 * SET, PEERS)
            send_weights(0)

        @pl.when(i == 2)
        def _():
            send_weights(1)

        @pl.when(i == 5)
        def _():
            wait_weights(0)
            send_weights(2)

        @pl.when(i > 0)
        def _():
            relay(i - 1)

    relay(SETS - 1)

    for n in (1, 2):
        wait_weights(n)

    @pl.loop(1, PEERS)
    def _(k):
        for n in range(3):
            w_wait(n, k)
        row_copy(k).wait_send()
        g_copy(k).wait_send()

    blocks = quarter // 128

    def weight(n, first, count):
        return wv[pl.ds(first, count), pl.ds(n * 128, 128), :].reshape(count * 128, cols)

    def hidden_rows(n, first, count):
        return pool[pl.ds(n * SETS + first, count)].reshape(count * SROWS, cols)

    def partial(i, j, h):
        da, db = hidden_rows(0, i * PER, PER), hidden_rows(1, i * PER, PER)
        first = j * blocks + h * (blocks // 2)
        value = lax.dot_general(
            da, weight(0, first, blocks // 2), over_last, preferred_element_type=F32
        ) + lax.dot_general(
            db, weight(1, first, blocks // 2), over_last, preferred_element_type=F32
        )
        return value.astype(BF16)

    row_at = lax.broadcasted_iota(jnp.int32, (SROWS, 128), 0)
    lane_at = lax.broadcasted_iota(jnp.int32, (SROWS, 128), 1)
    source_at = (
        (row_at >= CAP).astype(jnp.int32)
        + (row_at >= 2 * CAP).astype(jnp.int32)
        + (row_at >= 3 * CAP).astype(jnp.int32)
    )
    in_place = lane_at == row_at - source_at * CAP

    def s1_copies(i):
        return (
            th_copy(s1s.at[i % 2, 0], s1r.at[i, 0], s1_s.at[0, i], s1_r.at[0, i], right),
            th_copy(s1s.at[i % 2, 1], s1r.at[i, 1], s1_s.at[1, i], s1_r.at[1, i], left),
        )

    def s2_copies(i):
        return (
            th_copy(s2s.at[i, 0, 0], s2r.at[i, 0, 0], s2_s.at[0, i], s2_r.at[0, i], right),
            th_copy(s2s.at[i, 1, 1], s2r.at[i, 1, 1], s2_s.at[1, i], s2_r.at[1, i], left),
        )

    def d_copies(i):
        return (
            th_copy(s2s.at[i, 0, 1], s2r.at[i, 0, 1], d_s.at[0, i], d_r.at[0, i], right),
            th_copy(s2s.at[i, 1, 0], s2r.at[i, 1, 0], d_s.at[1, i], d_r.at[1, i], left),
        )

    def b_copy(k):
        return ep_copy(
            rr.at[k, :, pl.ds(0, strip)], back_ref.at[k], b_s.at[k], b_r.at[k], peer_from(me, k)
        )

    b_own = pltpu.make_async_copy(rr.at[0, :, pl.ds(0, strip)], back_ref.at[0], b_r.at[0])

    def combine(i):
        for n, copy in enumerate(s1_copies(i)):
            copy.wait_recv()
            s2s[i, n, n] = (s2s[i, n, n].astype(F32) + s1r[i, n].astype(F32)).astype(BF16)
        for copy in s2_copies(i):
            copy.start()

    def finish(i):
        for copy in (*d_copies(i), *s2_copies(i)):
            copy.wait_recv()
        for part in range(PER):
            base = (i * PER + part) * SET
            at = pl.ds(part * SROWS, SROWS)
            packed = jnp.zeros((SET * SROWS, strip), F32)
            for c in range(4):
                h, span = c // 2, pl.ds(c % 2 * strip, strip)
                total = (
                    own[i % 3, h, at, span].astype(F32)
                    + s2r[i, 0, h, at, span].astype(F32)
                    + s2r[i, 1, h, at, span].astype(F32)
                ).astype(BF16)
                packed += lax.dot_general(
                    pack[c], total, over_rows, preferred_element_type=F32
                )
            rr[pl.ds(base, SET), :, pl.ds(0, strip)] = packed.astype(BF16).reshape(
                SET, SROWS, strip
            )
            for n in range(SET):
                k = base + n

                @pl.when(k > 0)
                def _():
                    b_copy(k).start()

                @pl.when(k == 0)
                def _():
                    b_own.start()

    qp[...] = jnp.zeros_like(qp)

    @pl.loop(0, CHUNKS)
    def _(i):
        for part in range(PER):
            v_wait(i * PER + part)
        acc[...] = jnp.zeros_like(acc)

        @pl.loop(0, 4)
        def _(j):
            x = xy[j, pl.ds(i * PER, PER), 0].reshape(CROWS, quarter)
            y = xy[j, pl.ds(i * PER, PER), 1].reshape(CROWS, quarter)
            first = j * blocks
            acc[0] += jnp.dot(x, weight(0, first, blocks), preferred_element_type=F32)
            acc[1] += jnp.dot(x, weight(1, first, blocks), preferred_element_type=F32)
            acc[2] += jnp.dot(y, weight(2, first, blocks), preferred_element_type=F32)

        for part in range(PER):
            s = i * PER + part
            at = pl.ds(part * SROWS, SROWS)
            gate = jnp.zeros((SROWS, 128), F32)
            for n in range(SET):
                one = gr[s * SET + n].astype(F32)[0:1, :]
                gate = jnp.where(in_place & (source_at == n), one, gate)
            g = jnp.sum(gate, axis=1, keepdims=True)
            a, b, u = acc[0, at], acc[1, at], acc[2, at]
            sig = jax.nn.sigmoid(a)
            silu = a * sig
            hidden = silu * b
            dh = g * u
            pool[0 * SETS + s] = (dh * b * sig * (1.0 + a * (1.0 - sig))).astype(BF16)
            pool[1 * SETS + s] = (dh * silu).astype(BF16)
            pool[2 * SETS + s] = (g * hidden).astype(BF16)
            q = jnp.sum(u * hidden, axis=1, keepdims=True)
            for n in range(SET):
                mine = jnp.where(in_place & (source_at == n), q, 0.0)
                qp[s, pl.ds(n, 1), :] = jnp.sum(mine, axis=0, keepdims=True)

        @pl.when(i > 1)
        def _():
            for copy in s1_copies(i - 2):
                copy.wait_send()

        s1s[i % 2, 0] = partial(i, opp, 0)
        s1s[i % 2, 1] = partial(i, opp, 1)
        for copy in s1_copies(i):
            copy.start()

        @pl.loop(0, 2)
        def _(h):
            s2s[i, 0, 1 - h] = partial(i, right, 1 - h)
            s2s[i, 1, h] = partial(i, left, h)

            @pl.when(h == 0)
            def _():
                for copy in d_copies(i):
                    copy.start()

            own[i % 3, h] = partial(i, th, h)

        @pl.when(i > 0)
        def _():
            combine(i - 1)

        @pl.when(i > 1)
        def _():
            finish(i - 2)

    combine(CHUNKS - 1)

    q_copies = tuple(
        th_copy(qp, qr.at[n], q_s.at[n], q_r.at[n], p) for n, p in enumerate((right, left, opp))
    )
    for copy in q_copies:
        copy.start()
    finish(CHUNKS - 2)

    tile = half // 128

    def out_copies(t):
        return tuple(
            pltpu.make_async_copy(
                bounce.at[t % 2, pl.ds(n * tile, tile)], gw_ref.at[n, pl.ds(t * tile, tile)],
                o_s.at[t % 2, n],
            )
            for n in range(3)
        )

    def weight_grads(t):
        @pl.when(t > 1)
        def _():
            for copy in out_copies(t - 2):
                copy.wait()

        span = pl.ds(pl.multiple_of(t % 2 * half, half), half)
        for n, kind in enumerate((0, 0, 1)):
            rows = xy[t // 2, :, kind, :, span].reshape(SETS * SROWS, half)
            hid = hidden_rows(n, 0, SETS)
            value = lax.dot_general(rows, hid, over_rows, preferred_element_type=F32)
            bounce[t % 2, pl.ds(n * tile, tile)] = value.astype(BF16).reshape(tile, 128, cols)
        for copy in out_copies(t):
            copy.start()

    pl.loop(0, 4)(weight_grads)

    finish(CHUNKS - 1)
    for copy in q_copies:
        copy.wait_recv()

    def qb_copy(k):
        return ep_copy(gs.at[k], qb.at[k], qb_s.at[k], qb_r.at[k], peer_from(me, k))

    qb_own = pltpu.make_async_copy(gs.at[0], qb.at[0], qb_r.at[0])
    for s in range(SETS):
        total = qp[s] + qr[0, s] + qr[1, s] + qr[2, s]
        for n in range(SET):
            gs[s * SET + n] = jnp.broadcast_to(total[n : n + 1, :], (16, 128)).astype(BF16)
    qb_own.start()

    @pl.loop(1, PEERS)
    def _(k):
        qb_copy(k).start()

    pl.loop(4, 8)(weight_grads)
    for t in (6, 7):
        for copy in out_copies(t):
            copy.wait()

    def load(k):
        return pltpu.make_async_copy(back_ref.at[k], rr.at[k, :, pl.ds(strip, strip)], l_s.at[k])

    b_own.wait()
    load(0).start()

    @pl.loop(1, PEERS)
    def _(k):
        b_copy(k).wait_recv()
        load(k).start()

    qb_own.wait()

    for m in range(2):
        acc[m, pl.ds(0, pair), pl.ds(0, strip)] = jnp.zeros((pair, strip), F32)

    @pl.loop(0, PEERS)
    def _(k):
        @pl.when(k > 0)
        def _():
            qb_copy(k).wait_recv()

        load(k).wait()
        chosen = one_hot(k)
        found = jnp.dot(qb[k], chosen[:128, :tok_count], preferred_element_type=F32)
        routed[pl.ds(k, 1), :] = found[0:1, :]
        for m in range(2):
            acc[m, pl.ds(0, pair), pl.ds(0, strip)] += lax.dot_general(
                chosen[:, m * pair : (m + 1) * pair], rr[k, :, pl.ds(strip, strip)], over_rows,
                preferred_element_type=F32,
            )

    for c in range(4):
        tok_out[:, pl.ds(c * strip, strip)] = acc[
            c // 2, pl.ds(c % 2 * tok_count, tok_count), pl.ds(0, strip)
        ].astype(BF16)
    terms = routed[...]
    for n in range(top_count):
        same = routing_ref[pl.ds(n, 1), :] == expert
        gates_out[pl.ds(n, 1), :] = jnp.sum(jnp.where(same, terms, 0.0), axis=0, keepdims=True)

    @pl.loop(1, PEERS)
    def _(k):
        b_copy(k).wait_send()
        qb_copy(k).wait_send()

    for copy in q_copies:
        copy.wait_send()

    @pl.loop(0, SETS)
    def _(i):
        for copy in (*z_copies(i), *v_copies(i)):
            copy.wait_send()

    @pl.loop(0, CHUNKS)
    def _(i):
        for copy in (*d_copies(i), *s2_copies(i)):
            copy.wait_send()

    for i in (CHUNKS - 2, CHUNKS - 1):
        for copy in s1_copies(i):
            copy.wait_send()


def local(tokens, cotangent, gates, routing, new_slot, gate_old, up_old, down_old):
    tok_count, top_count = routing.shape
    quarter = tokens.shape[1]
    depth, cols = gate_old.shape[1:]
    ids = jnp.arange(PEERS, dtype=jnp.int32)
    expert = peer_to(lax.axis_index("ep"), ids)
    order = jnp.sum(
        (new_slot[None, :] == expert[:, None]).astype(jnp.int32) * ids[None, :], axis=1
    )
    half = quarter // 2
    strip = quarter // 4
    dma = pltpu.SemaphoreType.DMA
    peer, three = dma((PEERS,)), dma((3, PEERS))
    sets, ring = dma((2, SETS)), dma((2, CHUNKS))
    anywhere = pl.BlockSpec(memory_space=pl.ANY)
    inside = pl.BlockSpec(memory_space=pltpu.VMEM)
    grads, _, grad_tokens, grad_gates = pl.pallas_call(
        layer_body,
        out_shape=[
            jax.ShapeDtypeStruct((3, PEERS, depth, cols), BF16),
            jax.ShapeDtypeStruct((PEERS, SROWS, strip), BF16),
            jax.ShapeDtypeStruct(tokens.shape, BF16),
            jax.ShapeDtypeStruct((top_count, tok_count), F32),
        ],
        in_specs=[pl.BlockSpec(memory_space=pltpu.SMEM)] + [inside] * 5 + [anywhere] * 3,
        out_specs=[anywhere] * 2 + [inside] * 2,
        scratch_shapes=[
            pltpu.VMEM((PEERS, 3 * depth, cols), BF16),
            pltpu.VMEM((4, SETS, 2, SROWS, quarter), BF16),
            pltpu.VMEM((PEERS, SROWS, half), BF16),
            pltpu.VMEM((PEERS, 16, 128), BF16),
            pltpu.VMEM((PEERS, 16, 128), BF16),
            pltpu.VMEM((3, CROWS, cols), F32),
            pltpu.VMEM((2, 2, CROWS, half), BF16),
            pltpu.VMEM((CHUNKS, 2, CROWS, half), BF16),
            pltpu.VMEM((CHUNKS, 2, 2, CROWS, half), BF16),
            pltpu.VMEM((CHUNKS, 2, 2, CROWS, half), BF16),
            pltpu.VMEM((3, 2, CROWS, half), BF16),
            pltpu.VMEM((SETS, 8, 128), F32),
            pltpu.VMEM((3, SETS, 8, 128), F32),
            pltpu.VMEM((PEERS, 16, 128), BF16),
            pltpu.VMEM((PEERS, SROWS, cols), BF16),
            pltpu.VMEM((2, PEERS, depth, cols), BF16),
            pltpu.VMEM((4, SROWS, SET * SROWS), BF16),
            pltpu.VMEM((PEERS, 4 * tok_count), F32),
            pltpu.VMEM((PEERS, tok_count), F32),
            pltpu.VMEM((PEERS, tok_count), F32),
            peer, peer, peer, peer, three, three,
            sets, sets, sets, sets, ring, ring, ring, ring, ring, ring,
            peer, peer, dma((3,)), dma((3,)), peer, peer, dma((2, 3)), dma((3,)), peer,
        ],
        compiler_params=pltpu.CompilerParams(
            collective_id=0, has_side_effects=True, vmem_limit_bytes=63 * 2**20
        ),
    )(
        order, tokens, cotangent, gates.astype(F32).T, routing.T,
        jnp.broadcast_to(expert[:, None], (PEERS, tok_count)), gate_old, up_old, down_old,
    )
    grads = grads.reshape(3, PEERS * depth, cols)
    return (grad_tokens, grad_gates.T.astype(BF16), grads[0:1], grads[1:2], grads[2:3])


def solution(mesh):
    placed = (
        P("ep", "th"),
        P("ep", "th"),
        P("ep", None),
        P("ep", None),
        P(),
        P(None, "ep", "th"),
        P(None, "ep", "th"),
        P(None, "ep", "th"),
    )
    return jax.shard_map(
        local,
        mesh=mesh,
        in_specs=placed,
        out_specs=(
            P("ep", "th"),
            P("ep", None),
            P("ep", None, "th"),
            P("ep", None, "th"),
            P("ep", None, "th"),
        ),
        check_vma=False,
    )
```

```python
import jax
import jax.numpy as jnp
from jax import lax
from jax.experimental import pallas as pl
from jax.experimental.pallas import tpu as pltpu
from jax.sharding import PartitionSpec as P

CAP = 36
PEERS = 32
SET = 4
CHUNKS = 8
SETS = PEERS // SET
PER = SETS // CHUNKS
SROWS = SET * CAP
CROWS = PER * SROWS
MESH = pl.DeviceIdType.MESH
F32 = jnp.float32
BF16 = jnp.bfloat16


def offset(core, k):
    m, sign = k % 16, 1 + 2 * core
    return m % 4 * sign % 4, (m // 4 + m % 4) % 4 * sign % 4, k // 16


def peer_to(me, k):
    dx, dy, dc = offset(me % 2, k)
    return (me // 8 + dx) % 4 * 8 + ((me // 2) % 4 + dy) % 4 * 2 + (me % 2 + dc) % 2


def peer_from(me, k):
    core = (me % 2 + k // 16) % 2
    dx, dy, _ = offset(core, k)
    return (me // 8 + 4 - dx) % 4 * 8 + ((me // 2) % 4 + 4 - dy) % 4 * 2 + core


def layer_body(
    order_ref, tokens_ref, cot_ref, gates_ref, routing_ref, expert_ref, gate_ref, up_ref, down_ref,
    gw_ref, back_ref, tok_out, gates_out,
    wv, xy, rr, gr, gs, acc, s1s, s1r, s2s, s2r, own, qp, qr, qb, pool, bounce, pack,
    sums, spots, shares, routed,
    row_s, row_r, g_s, g_r, w_s, w_r, z_s, z_r, v_s, v_r, s1_s, s1_r, s2_s, s2_r, d_s, d_r,
    b_s, b_r, q_s, q_r, qb_s, qb_r, o_s, p_s, l_s,
):
    me = lax.axis_index("ep")
    th = lax.axis_index("th")
    right, left, opp = (th + 1) % 4, (th + 3) % 4, (th + 2) % 4
    cols = wv.shape[2]
    over_last = (((1,), (1,)), ((), ()))
    over_rows = (((0,), (0,)), ((), ()))

    def ep_copy(src, dst, s, r, p):
        return pltpu.make_async_remote_copy(
            src_ref=src, dst_ref=dst, send_sem=s, recv_sem=r, device_id={"ep": p},
            device_id_type=MESH,
        )

    def th_copy(src, dst, s, r, p):
        return pltpu.make_async_remote_copy(
            src_ref=src, dst_ref=dst, send_sem=s, recv_sem=r, device_id={"th": p},
            device_id_type=MESH,
        )

    barrier = pltpu.get_barrier_semaphore()

    @pl.loop(1, PEERS)
    def _(k):
        pl.semaphore_signal(
            barrier, inc=1, device_id={"ep": peer_to(me, k)}, device_id_type=MESH
        )

    for p in (right, left, opp):
        pl.semaphore_signal(barrier, inc=1, device_id={"th": p}, device_id_type=MESH)
    def pool_copy(n):
        return pltpu.make_async_copy((gate_ref, up_ref, down_ref)[n], pool.at[:, pl.ds(0, 128)], p_s.at[n])

    pool_copy(0).start()

    tok_count = tokens_ref.shape[0]
    quarter = tokens_ref.shape[1]
    half = quarter // 2
    strip = quarter // 4
    pair = 2 * tok_count
    top_count = routing_ref.shape[0]
    expert = expert_ref[...]
    hits = jnp.zeros((PEERS, tok_count), F32)
    share = jnp.zeros((PEERS, tok_count), F32)
    for n in range(top_count):
        same = routing_ref[pl.ds(n, 1), :] == expert
        hits = jnp.where(same, 1.0, hits)
        share = jnp.where(same, gates_ref[pl.ds(n, 1), :], share)
    earlier = lax.broadcasted_iota(jnp.int32, (tok_count, tok_count), 0) < (
        lax.broadcasted_iota(jnp.int32, (tok_count, tok_count), 1)
    )
    rank = jnp.dot(hits.astype(BF16), earlier.astype(F32).astype(BF16), preferred_element_type=F32)
    for c in range(4):
        spot = jnp.where(hits > 0.5, rank + float(c * CAP), -1.0)
        spots[:, pl.ds(c * tok_count, tok_count)] = spot
    shares[...] = share
    for c in range(2):
        at = pl.ds(c * half, half)
        own[0, c, pl.ds(0, tok_count), :] = tokens_ref[:, at]
        own[1, c, pl.ds(0, tok_count), :] = cot_ref[:, at]
    wide_row = lax.broadcasted_iota(jnp.int32, (SROWS, SET * SROWS), 0)
    wide_spot = lax.broadcasted_iota(jnp.int32, (SROWS, SET * SROWS), 1)
    for m in range(1, SET):
        wide_spot = wide_spot - jnp.where(wide_row >= m * CAP, SROWS - CAP, 0)
    for c in range(4):
        pack[c] = (wide_spot == wide_row + c * CAP).astype(F32).astype(BF16)
    row_ids = lax.broadcasted_iota(jnp.int32, (SROWS, 4 * tok_count), 0).astype(F32)

    def one_hot(k):
        return (row_ids == spots[pl.ds(k, 1), :]).astype(F32).astype(BF16)

    pl.semaphore_wait(barrier, PEERS - 1 + 3)

    def row_slot(k):
        return s2s.at[k // 4, k // 2 % 2, k % 2]

    def row_copy(k):
        return ep_copy(row_slot(k), rr.at[k], row_s.at[k], row_r.at[k], peer_to(me, k))

    def g_copy(k):
        return ep_copy(gs.at[k], gr.at[k], g_s.at[k], g_r.at[k], peer_to(me, k))

    def build(k):
        chosen = one_hot(k)
        held = own[pl.ds(0, 2), :, pl.ds(0, tok_count), :].reshape(4 * tok_count, half)
        block = jnp.dot(chosen, held, preferred_element_type=F32).astype(BF16)
        s2s[k // 4, k // 2 % 2, k % 2] = block
        mine = jnp.broadcast_to(shares[pl.ds(k, 1), :], (16, tok_count)).astype(BF16)
        gs[k] = lax.dot_general(
            mine, chosen[:128, :tok_count], over_last, preferred_element_type=F32
        ).astype(BF16)

    def w_copy(n, k):
        return ep_copy(
            bounce.at[n % 2, k], wv.at[me, pl.ds(n * 128, 128)], w_s.at[n, k], w_r.at[n, k],
            peer_to(me, k),
        )

    def w_wait(n, k):
        s = peer_from(me, k)
        ep_copy(
            bounce.at[n % 2, k], wv.at[s, pl.ds(n * 128, 128)], w_s.at[n, k], w_r.at[n, k], s
        ).wait_recv()

    def w_own(n):
        return pltpu.make_async_copy(
            bounce.at[n % 2, 0], wv.at[me, pl.ds(n * 128, 128)], w_r.at[n, 0]
        )

    def send_weights(n):
        pool_copy(n).wait()

        @pl.loop(0, PEERS)
        def _(k):
            bounce[n % 2, k] = pool[order_ref[k]][:128]

            @pl.when(k > 0)
            def _():
                w_copy(n, k).start()

        w_own(n).start()
        if n < 2:
            pool_copy(n + 1).start()

    def wait_weights(n):
        w_own(n).wait()

        @pl.loop(1, PEERS)
        def _(k):
            w_copy(n, k).wait_send()

    row_own = pltpu.make_async_copy(row_slot(0), rr.at[0], row_r.at[0])
    g_own = pltpu.make_async_copy(gs.at[0], gr.at[0], g_r.at[0])

    def send_rows(first, last):
        @pl.loop(first, last)
        def _(k):
            build(k)
            g_copy(k).start()
            row_copy(k).start()

    build(0)
    row_own.start()
    g_own.start()
    send_rows(1, 3 * SET)

    def z_copies(i):
        return (
            th_copy(xy.at[th, i], xy.at[th, i], z_s.at[0, i], z_r.at[0, i], right),
            th_copy(xy.at[th, i], xy.at[th, i], z_s.at[1, i], z_r.at[1, i], left),
        )

    def z_wait(i):
        th_copy(xy.at[left, i], xy.at[left, i], z_s.at[0, i], z_r.at[0, i], left).wait_recv()
        th_copy(xy.at[right, i], xy.at[right, i], z_s.at[1, i], z_r.at[1, i], right).wait_recv()

    def v_copies(i):
        return (
            th_copy(xy.at[left, i, 0], xy.at[left, i, 0], v_s.at[0, i], v_r.at[0, i], right),
            th_copy(xy.at[right, i, 1], xy.at[right, i, 1], v_s.at[1, i], v_r.at[1, i], left),
        )

    def v_wait(i):
        th_copy(xy.at[opp, i, 0], xy.at[opp, i, 0], v_s.at[0, i], v_r.at[0, i], left).wait_recv()
        th_copy(xy.at[opp, i, 1], xy.at[opp, i, 1], v_s.at[1, i], v_r.at[1, i], right).wait_recv()

    def relay(i):
        z_wait(i)
        for copy in v_copies(i):
            copy.start()

    row_own.wait()
    g_own.wait()

    @pl.loop(0, SETS)
    def _(i):
        for n in range(SET):
            k = i * SET + n

            @pl.when(k > 0)
            def _():
                row_copy(k).wait_recv()
                g_copy(k).wait_recv()

        @pl.when(i == 0)
        def _():
            send_rows(3 * SET, 6 * SET)

        arrived = rr[pl.ds(i * SET, SET)].reshape(SET * SROWS, rr.shape[2])
        wide = rr.shape[2]
        for c in range(4):
            piece = jnp.dot(pack[c], arrived, preferred_element_type=F32).astype(BF16)
            xy[th, i, c // 2, :, pl.ds(c % 2 * wide, wide)] = piece
        for copy in z_copies(i):
            copy.start()

        @pl.when(i == 1)
        def _():
            send_rows(6 * SET, PEERS)
            send_weights(0)

        @pl.when(i == 2)
        def _():
            send_weights(1)

        @pl.when(i == 5)
        def _():
            wait_weights(0)
            send_weights(2)

        @pl.when(i > 0)
        def _():
            relay(i - 1)

    relay(SETS - 1)

    for n in (1, 2):
        wait_weights(n)

    @pl.loop(1, PEERS)
    def _(k):
        for n in range(3):
            w_wait(n, k)
        row_copy(k).wait_send()
        g_copy(k).wait_send()

    blocks = quarter // 128

    def weight(n, first, count):
        return wv[pl.ds(first, count), pl.ds(n * 128, 128), :].reshape(count * 128, cols)

    def hidden_rows(n, first, count):
        return pool[pl.ds(n * SETS + first, count)].reshape(count * SROWS, cols)

    def partial(i, j, h):
        da, db = hidden_rows(0, i * PER, PER), hidden_rows(1, i * PER, PER)
        first = j * blocks + h * (blocks // 2)
        value = lax.dot_general(
            da, weight(0, first, blocks // 2), over_last, preferred_element_type=F32
        ) + lax.dot_general(
            db, weight(1, first, blocks // 2), over_last, preferred_element_type=F32
        )
        return value.astype(BF16)

    row_at = lax.broadcasted_iota(jnp.int32, (SROWS, 128), 0)
    lane_at = lax.broadcasted_iota(jnp.int32, (SROWS, 128), 1)
    source_at = (
        (row_at >= CAP).astype(jnp.int32)
        + (row_at >= 2 * CAP).astype(jnp.int32)
        + (row_at >= 3 * CAP).astype(jnp.int32)
    )
    in_place = lane_at == row_at - source_at * CAP

    def s1_copies(i):
        return (
            th_copy(s1s.at[i % 2, 0], s1r.at[i, 0], s1_s.at[0, i], s1_r.at[0, i], right),
            th_copy(s1s.at[i % 2, 1], s1r.at[i, 1], s1_s.at[1, i], s1_r.at[1, i], left),
        )

    def s2_copies(i):
        return (
            th_copy(s2s.at[i, 0, 0], s2r.at[i, 0, 0], s2_s.at[0, i], s2_r.at[0, i], right),
            th_copy(s2s.at[i, 1, 1], s2r.at[i, 1, 1], s2_s.at[1, i], s2_r.at[1, i], left),
        )

    def d_copies(i):
        return (
            th_copy(s2s.at[i, 0, 1], s2r.at[i, 0, 1], d_s.at[0, i], d_r.at[0, i], right),
            th_copy(s2s.at[i, 1, 0], s2r.at[i, 1, 0], d_s.at[1, i], d_r.at[1, i], left),
        )

    def b_copy(k):
        return ep_copy(
            rr.at[k, :, pl.ds(0, strip)], back_ref.at[k], b_s.at[k], b_r.at[k], peer_from(me, k)
        )

    b_own = pltpu.make_async_copy(rr.at[0, :, pl.ds(0, strip)], back_ref.at[0], b_r.at[0])

    def combine(i):
        for n, copy in enumerate(s1_copies(i)):
            copy.wait_recv()
            s2s[i, n, n] = (s2s[i, n, n].astype(F32) + s1r[i, n].astype(F32)).astype(BF16)
        for copy in s2_copies(i):
            copy.start()

    def finish(i):
        for copy in (*d_copies(i), *s2_copies(i)):
            copy.wait_recv()
        for part in range(PER):
            base = (i * PER + part) * SET
            at = pl.ds(part * SROWS, SROWS)
            packed = jnp.zeros((SET * SROWS, strip), F32)
            for c in range(4):
                h, span = c // 2, pl.ds(c % 2 * strip, strip)
                total = (
                    own[i % 3, h, at, span].astype(F32)
                    + s2r[i, 0, h, at, span].astype(F32)
                    + s2r[i, 1, h, at, span].astype(F32)
                ).astype(BF16)
                packed += lax.dot_general(
                    pack[c], total, over_rows, preferred_element_type=F32
                )
            rr[pl.ds(base, SET), :, pl.ds(0, strip)] = packed.astype(BF16).reshape(
                SET, SROWS, strip
            )
            for n in range(SET):
                k = base + n

                @pl.when(k > 0)
                def _():
                    b_copy(k).start()

                @pl.when(k == 0)
                def _():
                    b_own.start()

    qp[...] = jnp.zeros_like(qp)

    @pl.loop(0, CHUNKS)
    def _(i):
        for part in range(PER):
            v_wait(i * PER + part)
        acc[...] = jnp.zeros_like(acc)

        @pl.loop(0, 4)
        def _(j):
            x = xy[j, pl.ds(i * PER, PER), 0].reshape(CROWS, quarter)
            y = xy[j, pl.ds(i * PER, PER), 1].reshape(CROWS, quarter)
            first = j * blocks
            acc[0] += jnp.dot(x, weight(0, first, blocks), preferred_element_type=F32)
            acc[1] += jnp.dot(x, weight(1, first, blocks), preferred_element_type=F32)
            acc[2] += jnp.dot(y, weight(2, first, blocks), preferred_element_type=F32)

        for part in range(PER):
            s = i * PER + part
            at = pl.ds(part * SROWS, SROWS)
            gate = jnp.zeros((SROWS, 128), F32)
            for n in range(SET):
                one = gr[s * SET + n].astype(F32)[0:1, :]
                gate = jnp.where(in_place & (source_at == n), one, gate)
            g = jnp.sum(gate, axis=1, keepdims=True)
            a, b, u = acc[0, at], acc[1, at], acc[2, at]
            sig = jax.nn.sigmoid(a)
            silu = a * sig
            hidden = silu * b
            dh = g * u
            pool[0 * SETS + s] = (dh * b * sig * (1.0 + a * (1.0 - sig))).astype(BF16)
            pool[1 * SETS + s] = (dh * silu).astype(BF16)
            pool[2 * SETS + s] = (g * hidden).astype(BF16)
            q = jnp.sum(u * hidden, axis=1, keepdims=True)
            for n in range(SET):
                mine = jnp.where(in_place & (source_at == n), q, 0.0)
                qp[s, pl.ds(n, 1), :] = jnp.sum(mine, axis=0, keepdims=True)

        @pl.when(i > 1)
        def _():
            for copy in s1_copies(i - 2):
                copy.wait_send()

        s1s[i % 2, 0] = partial(i, opp, 0)
        s1s[i % 2, 1] = partial(i, opp, 1)
        for copy in s1_copies(i):
            copy.start()

        @pl.loop(0, 2)
        def _(h):
            s2s[i, 0, 1 - h] = partial(i, right, 1 - h)
            s2s[i, 1, h] = partial(i, left, h)

            @pl.when(h == 0)
            def _():
                for copy in d_copies(i):
                    copy.start()

            own[i % 3, h] = partial(i, th, h)

        @pl.when(i > 0)
        def _():
            combine(i - 1)

        @pl.when(i > 1)
        def _():
            finish(i - 2)

    q_copies = tuple(
        th_copy(qp, qr.at[n], q_s.at[n], q_r.at[n], p) for n, p in enumerate((right, left, opp))
    )
    for copy in q_copies:
        copy.start()

    tile = half // 128

    def out_copies(t):
        return tuple(
            pltpu.make_async_copy(
                bounce.at[t % 2, pl.ds(n * tile, tile)], gw_ref.at[n, pl.ds(t * tile, tile)],
                o_s.at[t % 2, n],
            )
            for n in range(3)
        )

    def weight_grads(t):
        @pl.when(t > 1)
        def _():
            for copy in out_copies(t - 2):
                copy.wait()

        span = pl.ds(pl.multiple_of(t % 2 * half, half), half)
        for n, kind in enumerate((0, 0, 1)):
            rows = xy[t // 2, :, kind, :, span].reshape(SETS * SROWS, half)
            hid = hidden_rows(n, 0, SETS)
            value = lax.dot_general(rows, hid, over_rows, preferred_element_type=F32)
            bounce[t % 2, pl.ds(n * tile, tile)] = value.astype(BF16).reshape(tile, 128, cols)
        for copy in out_copies(t):
            copy.start()

    pl.loop(0, 4)(weight_grads)
    combine(CHUNKS - 1)
    finish(CHUNKS - 2)
    pl.loop(4, 6)(weight_grads)

    for copy in q_copies:
        copy.wait_recv()

    def qb_copy(k):
        return ep_copy(gs.at[k], qb.at[k], qb_s.at[k], qb_r.at[k], peer_from(me, k))

    qb_own = pltpu.make_async_copy(gs.at[0], qb.at[0], qb_r.at[0])
    for s in range(SETS):
        total = qp[s] + qr[0, s] + qr[1, s] + qr[2, s]
        for n in range(SET):
            gs[s * SET + n] = jnp.broadcast_to(total[n : n + 1, :], (16, 128)).astype(BF16)
    qb_own.start()

    @pl.loop(1, PEERS)
    def _(k):
        qb_copy(k).start()

    def load(k):
        return pltpu.make_async_copy(back_ref.at[k], rr.at[k, :, pl.ds(strip, strip)], l_s.at[k])

    qb_own.wait()

    for m in range(2):
        sums[m] = jnp.zeros((pair, strip), F32)

    def sum_tokens(first, last):
        @pl.loop(first, last)
        def _(k):
            @pl.when(k > 0)
            def _():
                b_copy(k).wait_recv()

            @pl.when(k == 0)
            def _():
                b_own.wait()

            load(k).start()

        @pl.loop(first, last)
        def _(k):
            @pl.when(k > 0)
            def _():
                qb_copy(k).wait_recv()

            load(k).wait()
            chosen = one_hot(k)
            found = jnp.dot(qb[k], chosen[:128, :tok_count], preferred_element_type=F32)
            routed[pl.ds(k, 1), :] = found[0:1, :]
            for m in range(2):
                sums[m] += lax.dot_general(
                    chosen[:, m * pair : (m + 1) * pair], rr[k, :, pl.ds(strip, strip)], over_rows,
                    preferred_element_type=F32,
                )

    sum_tokens(0, PEERS // 2)
    finish(CHUNKS - 1)
    pl.loop(6, 8)(weight_grads)
    for t in (6, 7):
        for copy in out_copies(t):
            copy.wait()

    sum_tokens(PEERS // 2, PEERS)
    for c in range(4):
        tok_out[:, pl.ds(c * strip, strip)] = sums[
            c // 2, pl.ds(c % 2 * tok_count, tok_count)
        ].astype(BF16)
    terms = routed[...]
    for n in range(top_count):
        same = routing_ref[pl.ds(n, 1), :] == expert
        gates_out[pl.ds(n, 1), :] = jnp.sum(jnp.where(same, terms, 0.0), axis=0, keepdims=True)

    @pl.loop(1, PEERS)
    def _(k):
        b_copy(k).wait_send()
        qb_copy(k).wait_send()

    for copy in q_copies:
        copy.wait_send()

    @pl.loop(0, SETS)
    def _(i):
        for copy in (*z_copies(i), *v_copies(i)):
            copy.wait_send()

    @pl.loop(0, CHUNKS)
    def _(i):
        for copy in (*d_copies(i), *s2_copies(i)):
            copy.wait_send()

    for i in (CHUNKS - 2, CHUNKS - 1):
        for copy in s1_copies(i):
            copy.wait_send()


def local(tokens, cotangent, gates, routing, new_slot, gate_old, up_old, down_old):
    tok_count, top_count = routing.shape
    quarter = tokens.shape[1]
    depth, cols = gate_old.shape[1:]
    ids = jnp.arange(PEERS, dtype=jnp.int32)
    expert = peer_to(lax.axis_index("ep"), ids)
    order = jnp.sum(
        (new_slot[None, :] == expert[:, None]).astype(jnp.int32) * ids[None, :], axis=1
    )
    half = quarter // 2
    strip = quarter // 4
    dma = pltpu.SemaphoreType.DMA
    peer, three = dma((PEERS,)), dma((3, PEERS))
    sets, ring = dma((2, SETS)), dma((2, CHUNKS))
    anywhere = pl.BlockSpec(memory_space=pl.ANY)
    inside = pl.BlockSpec(memory_space=pltpu.VMEM)
    grads, _, grad_tokens, grad_gates = pl.pallas_call(
        layer_body,
        out_shape=[
            jax.ShapeDtypeStruct((3, PEERS, depth, cols), BF16),
            jax.ShapeDtypeStruct((PEERS, SROWS, strip), BF16),
            jax.ShapeDtypeStruct(tokens.shape, BF16),
            jax.ShapeDtypeStruct((top_count, tok_count), F32),
        ],
        in_specs=[pl.BlockSpec(memory_space=pltpu.SMEM)] + [inside] * 5 + [anywhere] * 3,
        out_specs=[anywhere] * 2 + [inside] * 2,
        scratch_shapes=[
            pltpu.VMEM((PEERS, 3 * depth, cols), BF16),
            pltpu.VMEM((4, SETS, 2, SROWS, quarter), BF16),
            pltpu.VMEM((PEERS, SROWS, half), BF16),
            pltpu.VMEM((PEERS, 16, 128), BF16),
            pltpu.VMEM((PEERS, 16, 128), BF16),
            pltpu.VMEM((3, CROWS, cols), F32),
            pltpu.VMEM((2, 2, CROWS, half), BF16),
            pltpu.VMEM((CHUNKS, 2, CROWS, half), BF16),
            pltpu.VMEM((CHUNKS, 2, 2, CROWS, half), BF16),
            pltpu.VMEM((CHUNKS, 2, 2, CROWS, half), BF16),
            pltpu.VMEM((3, 2, CROWS, half), BF16),
            pltpu.VMEM((SETS, 8, 128), F32),
            pltpu.VMEM((3, SETS, 8, 128), F32),
            pltpu.VMEM((PEERS, 16, 128), BF16),
            pltpu.VMEM((PEERS, SROWS, cols), BF16),
            pltpu.VMEM((2, PEERS, depth, cols), BF16),
            pltpu.VMEM((4, SROWS, SET * SROWS), BF16),
            pltpu.VMEM((2, 2 * tok_count, strip), F32),
            pltpu.VMEM((PEERS, 4 * tok_count), F32),
            pltpu.VMEM((PEERS, tok_count), F32),
            pltpu.VMEM((PEERS, tok_count), F32),
            peer, peer, peer, peer, three, three,
            sets, sets, sets, sets, ring, ring, ring, ring, ring, ring,
            peer, peer, dma((3,)), dma((3,)), peer, peer, dma((2, 3)), dma((3,)), peer,
        ],
        compiler_params=pltpu.CompilerParams(
            collective_id=0, has_side_effects=True, vmem_limit_bytes=63 * 2**20
        ),
    )(
        order, tokens, cotangent, gates.astype(F32).T, routing.T,
        jnp.broadcast_to(expert[:, None], (PEERS, tok_count)), gate_old, up_old, down_old,
    )
    grads = grads.reshape(3, PEERS * depth, cols)
    return (grad_tokens, grad_gates.T.astype(BF16), grads[0:1], grads[1:2], grads[2:3])


def solution(mesh):
    placed = (
        P("ep", "th"),
        P("ep", "th"),
        P("ep", None),
        P("ep", None),
        P(),
        P(None, "ep", "th"),
        P(None, "ep", "th"),
        P(None, "ep", "th"),
    )
    return jax.shard_map(
        local,
        mesh=mesh,
        in_specs=placed,
        out_specs=(
            P("ep", "th"),
            P("ep", None),
            P("ep", None, "th"),
            P("ep", None, "th"),
            P("ep", None, "th"),
        ),
        check_vma=False,
    )
```

```python
import jax
import jax.numpy as jnp
from jax import lax
from jax.experimental import pallas as pl
from jax.experimental.pallas import tpu as pltpu
from jax.sharding import PartitionSpec as P

CAP = 36
PEERS = 32
SET = 4
CHUNKS = 8
SETS = PEERS // SET
PER = SETS // CHUNKS
SROWS = SET * CAP
CROWS = PER * SROWS
MESH = pl.DeviceIdType.MESH
F32 = jnp.float32
BF16 = jnp.bfloat16


def offset(core, k):
    m, sign = k % 16, 1 + 2 * core
    return m % 4 * sign % 4, (m // 4 + m % 4) % 4 * sign % 4, k // 16


def peer_to(me, k):
    dx, dy, dc = offset(me % 2, k)
    return (me // 8 + dx) % 4 * 8 + ((me // 2) % 4 + dy) % 4 * 2 + (me % 2 + dc) % 2


def peer_from(me, k):
    core = (me % 2 + k // 16) % 2
    dx, dy, _ = offset(core, k)
    return (me // 8 + 4 - dx) % 4 * 8 + ((me // 2) % 4 + 4 - dy) % 4 * 2 + core


def layer_body(
    order_ref, tokens_ref, cot_ref, gates_ref, routing_ref, expert_ref, gate_ref, up_ref, down_ref,
    gw_ref, back_ref, tok_out, gates_out,
    wv, xy, rr, gr, gs, acc, s1s, s1r, s2s, s2r, own, qp, qr, qb, pool, bounce, pack,
    sums, spots, shares, routed,
    row_s, row_r, g_s, g_r, w_s, w_r, z_s, z_r, v_s, v_r, s1_s, s1_r, s2_s, s2_r, d_s, d_r,
    b_s, b_r, q_s, q_r, qb_s, qb_r, o_s, p_s, l_s,
):
    me = lax.axis_index("ep")
    th = lax.axis_index("th")
    right, left, opp = (th + 1) % 4, (th + 3) % 4, (th + 2) % 4
    cols = wv.shape[2]
    over_last = (((1,), (1,)), ((), ()))
    over_rows = (((0,), (0,)), ((), ()))

    def ep_copy(src, dst, s, r, p):
        return pltpu.make_async_remote_copy(
            src_ref=src, dst_ref=dst, send_sem=s, recv_sem=r, device_id={"ep": p},
            device_id_type=MESH,
        )

    def th_copy(src, dst, s, r, p):
        return pltpu.make_async_remote_copy(
            src_ref=src, dst_ref=dst, send_sem=s, recv_sem=r, device_id={"th": p},
            device_id_type=MESH,
        )

    barrier = pltpu.get_barrier_semaphore()

    @pl.loop(1, PEERS)
    def _(k):
        pl.semaphore_signal(
            barrier, inc=1, device_id={"ep": peer_to(me, k)}, device_id_type=MESH
        )

    for p in (right, left, opp):
        pl.semaphore_signal(barrier, inc=1, device_id={"th": p}, device_id_type=MESH)
    def pool_copy(n):
        return pltpu.make_async_copy((gate_ref, up_ref, down_ref)[n], pool.at[:, pl.ds(0, 128)], p_s.at[n])

    pool_copy(0).start()

    tok_count = tokens_ref.shape[0]
    quarter = tokens_ref.shape[1]
    half = quarter // 2
    strip = quarter // 4
    pair = 2 * tok_count
    top_count = routing_ref.shape[0]
    expert = expert_ref[...]
    hits = jnp.zeros((PEERS, tok_count), F32)
    share = jnp.zeros((PEERS, tok_count), F32)
    for n in range(top_count):
        same = routing_ref[pl.ds(n, 1), :] == expert
        hits = jnp.where(same, 1.0, hits)
        share = jnp.where(same, gates_ref[pl.ds(n, 1), :], share)
    earlier = lax.broadcasted_iota(jnp.int32, (tok_count, tok_count), 0) < (
        lax.broadcasted_iota(jnp.int32, (tok_count, tok_count), 1)
    )
    rank = jnp.dot(hits.astype(BF16), earlier.astype(F32).astype(BF16), preferred_element_type=F32)
    for c in range(4):
        spot = jnp.where(hits > 0.5, rank + float(c * CAP), -1.0)
        spots[:, pl.ds(c * tok_count, tok_count)] = spot
    shares[...] = share
    for c in range(2):
        at = pl.ds(c * half, half)
        own[0, c, pl.ds(0, tok_count), :] = tokens_ref[:, at]
        own[1, c, pl.ds(0, tok_count), :] = cot_ref[:, at]
    wide_row = lax.broadcasted_iota(jnp.int32, (SROWS, SET * SROWS), 0)
    wide_spot = lax.broadcasted_iota(jnp.int32, (SROWS, SET * SROWS), 1)
    for m in range(1, SET):
        wide_spot = wide_spot - jnp.where(wide_row >= m * CAP, SROWS - CAP, 0)
    for c in range(4):
        pack[c] = (wide_spot == wide_row + c * CAP).astype(F32).astype(BF16)
    row_ids = lax.broadcasted_iota(jnp.int32, (SROWS, 4 * tok_count), 0).astype(F32)

    def one_hot(k):
        return (row_ids == spots[pl.ds(k, 1), :]).astype(F32).astype(BF16)

    pl.semaphore_wait(barrier, PEERS - 1 + 3)

    def row_slot(k):
        return s2s.at[k // 4, k // 2 % 2, k % 2]

    def row_copy(k):
        return ep_copy(row_slot(k), rr.at[k], row_s.at[k], row_r.at[k], peer_to(me, k))

    def g_copy(k):
        return ep_copy(gs.at[k], gr.at[k], g_s.at[k], g_r.at[k], peer_to(me, k))

    def build(k):
        chosen = one_hot(k)
        held = own[pl.ds(0, 2), :, pl.ds(0, tok_count), :].reshape(4 * tok_count, half)
        block = jnp.dot(chosen, held, preferred_element_type=F32).astype(BF16)
        s2s[k // 4, k // 2 % 2, k % 2] = block
        mine = jnp.broadcast_to(shares[pl.ds(k, 1), :], (16, tok_count)).astype(BF16)
        gs[k] = lax.dot_general(
            mine, chosen[:128, :tok_count], over_last, preferred_element_type=F32
        ).astype(BF16)

    def w_copy(n, k):
        return ep_copy(
            bounce.at[n % 2, k], wv.at[me, pl.ds(n * 128, 128)], w_s.at[n, k], w_r.at[n, k],
            peer_to(me, k),
        )

    def w_wait(n, k):
        s = peer_from(me, k)
        ep_copy(
            bounce.at[n % 2, k], wv.at[s, pl.ds(n * 128, 128)], w_s.at[n, k], w_r.at[n, k], s
        ).wait_recv()

    def w_own(n):
        return pltpu.make_async_copy(
            bounce.at[n % 2, 0], wv.at[me, pl.ds(n * 128, 128)], w_r.at[n, 0]
        )

    def send_weights(n):
        pool_copy(n).wait()

        @pl.loop(0, PEERS)
        def _(k):
            bounce[n % 2, k] = pool[order_ref[k]][:128]

            @pl.when(k > 0)
            def _():
                w_copy(n, k).start()

        w_own(n).start()
        if n < 2:
            pool_copy(n + 1).start()

    def wait_weights(n):
        w_own(n).wait()

        @pl.loop(1, PEERS)
        def _(k):
            w_copy(n, k).wait_send()

    row_own = pltpu.make_async_copy(row_slot(0), rr.at[0], row_r.at[0])
    g_own = pltpu.make_async_copy(gs.at[0], gr.at[0], g_r.at[0])

    def send_rows(first, last):
        @pl.loop(first, last)
        def _(k):
            build(k)
            g_copy(k).start()
            row_copy(k).start()

    build(0)
    row_own.start()
    g_own.start()
    send_rows(1, 3 * SET)

    def z_copies(i):
        return (
            th_copy(xy.at[th, i], xy.at[th, i], z_s.at[0, i], z_r.at[0, i], right),
            th_copy(xy.at[th, i], xy.at[th, i], z_s.at[1, i], z_r.at[1, i], left),
        )

    def z_wait(i):
        th_copy(xy.at[left, i], xy.at[left, i], z_s.at[0, i], z_r.at[0, i], left).wait_recv()
        th_copy(xy.at[right, i], xy.at[right, i], z_s.at[1, i], z_r.at[1, i], right).wait_recv()

    def v_copies(i):
        return (
            th_copy(xy.at[left, i, 0], xy.at[left, i, 0], v_s.at[0, i], v_r.at[0, i], right),
            th_copy(xy.at[right, i, 1], xy.at[right, i, 1], v_s.at[1, i], v_r.at[1, i], left),
        )

    def v_wait(i):
        th_copy(xy.at[opp, i, 0], xy.at[opp, i, 0], v_s.at[0, i], v_r.at[0, i], left).wait_recv()
        th_copy(xy.at[opp, i, 1], xy.at[opp, i, 1], v_s.at[1, i], v_r.at[1, i], right).wait_recv()

    def relay(i):
        z_wait(i)
        for copy in v_copies(i):
            copy.start()

    row_own.wait()
    g_own.wait()

    @pl.loop(0, SETS)
    def _(i):
        for n in range(SET):
            k = i * SET + n

            @pl.when(k > 0)
            def _():
                row_copy(k).wait_recv()
                g_copy(k).wait_recv()

        @pl.when(i == 0)
        def _():
            send_rows(3 * SET, 6 * SET)

        arrived = rr[pl.ds(i * SET, SET)].reshape(SET * SROWS, rr.shape[2])
        wide = rr.shape[2]
        for c in range(4):
            piece = jnp.dot(pack[c], arrived, preferred_element_type=F32).astype(BF16)
            xy[th, i, c // 2, :, pl.ds(c % 2 * wide, wide)] = piece
        for copy in z_copies(i):
            copy.start()

        @pl.when(i == 1)
        def _():
            send_rows(6 * SET, PEERS)
            send_weights(0)

        @pl.when(i == 2)
        def _():
            send_weights(1)

        @pl.when(i == 5)
        def _():
            wait_weights(0)
            send_weights(2)

        @pl.when(i > 0)
        def _():
            relay(i - 1)

    relay(SETS - 1)

    for n in (1, 2):
        wait_weights(n)

    @pl.loop(1, PEERS)
    def _(k):
        for n in range(3):
            w_wait(n, k)
        row_copy(k).wait_send()
        g_copy(k).wait_send()

    blocks = quarter // 128

    def weight(n, first, count):
        return wv[pl.ds(first, count), pl.ds(n * 128, 128), :].reshape(count * 128, cols)

    def hidden_rows(n, first, count):
        return pool[pl.ds(n * SETS + first, count)].reshape(count * SROWS, cols)

    def partial(i, j, h):
        da, db = hidden_rows(0, i * PER, PER), hidden_rows(1, i * PER, PER)
        first = j * blocks + h * (blocks // 2)
        value = lax.dot_general(
            da, weight(0, first, blocks // 2), over_last, preferred_element_type=F32
        ) + lax.dot_general(
            db, weight(1, first, blocks // 2), over_last, preferred_element_type=F32
        )
        return value.astype(BF16)

    row_at = lax.broadcasted_iota(jnp.int32, (SROWS, 128), 0)
    lane_at = lax.broadcasted_iota(jnp.int32, (SROWS, 128), 1)
    source_at = (
        (row_at >= CAP).astype(jnp.int32)
        + (row_at >= 2 * CAP).astype(jnp.int32)
        + (row_at >= 3 * CAP).astype(jnp.int32)
    )
    in_place = lane_at == row_at - source_at * CAP

    def s1_copies(i):
        return (
            th_copy(s1s.at[i % 2, 0], s1r.at[i, 0], s1_s.at[0, i], s1_r.at[0, i], right),
            th_copy(s1s.at[i % 2, 1], s1r.at[i, 1], s1_s.at[1, i], s1_r.at[1, i], left),
        )

    def s2_copies(i):
        return (
            th_copy(s2s.at[i, 0, 0], s2r.at[i, 0, 0], s2_s.at[0, i], s2_r.at[0, i], right),
            th_copy(s2s.at[i, 1, 1], s2r.at[i, 1, 1], s2_s.at[1, i], s2_r.at[1, i], left),
        )

    def d_copies(i):
        return (
            th_copy(s2s.at[i, 0, 1], s2r.at[i, 0, 1], d_s.at[0, i], d_r.at[0, i], right),
            th_copy(s2s.at[i, 1, 0], s2r.at[i, 1, 0], d_s.at[1, i], d_r.at[1, i], left),
        )

    def b_copy(k):
        return ep_copy(
            rr.at[k, :, pl.ds(0, strip)], back_ref.at[k], b_s.at[k], b_r.at[k], peer_from(me, k)
        )

    b_own = pltpu.make_async_copy(rr.at[0, :, pl.ds(0, strip)], back_ref.at[0], b_r.at[0])

    def combine(i):
        for n, copy in enumerate(s1_copies(i)):
            copy.wait_recv()
            s2s[i, n, n] = (s2s[i, n, n].astype(F32) + s1r[i, n].astype(F32)).astype(BF16)
        for copy in s2_copies(i):
            copy.start()

    def finish(i):
        for copy in (*d_copies(i), *s2_copies(i)):
            copy.wait_recv()
        for part in range(PER):
            base = (i * PER + part) * SET
            at = pl.ds(part * SROWS, SROWS)
            packed = jnp.zeros((SET * SROWS, strip), F32)
            for c in range(4):
                h, span = c // 2, pl.ds(c % 2 * strip, strip)
                total = (
                    own[i % 3, h, at, span].astype(F32)
                    + s2r[i, 0, h, at, span].astype(F32)
                    + s2r[i, 1, h, at, span].astype(F32)
                ).astype(BF16)
                packed += lax.dot_general(
                    pack[c], total, over_rows, preferred_element_type=F32
                )
            rr[pl.ds(base, SET), :, pl.ds(0, strip)] = packed.astype(BF16).reshape(
                SET, SROWS, strip
            )
            for n in range(SET):
                k = base + n

                @pl.when(k > 0)
                def _():
                    b_copy(k).start()

                @pl.when(k == 0)
                def _():
                    b_own.start()

    qp[...] = jnp.zeros_like(qp)

    @pl.loop(0, CHUNKS)
    def _(i):
        for part in range(PER):
            v_wait(i * PER + part)
        acc[...] = jnp.zeros_like(acc)

        @pl.loop(0, 4)
        def _(j):
            x = xy[j, pl.ds(i * PER, PER), 0].reshape(CROWS, quarter)
            y = xy[j, pl.ds(i * PER, PER), 1].reshape(CROWS, quarter)
            first = j * blocks
            acc[0] += jnp.dot(x, weight(0, first, blocks), preferred_element_type=F32)
            acc[1] += jnp.dot(x, weight(1, first, blocks), preferred_element_type=F32)
            acc[2] += jnp.dot(y, weight(2, first, blocks), preferred_element_type=F32)

        for part in range(PER):
            s = i * PER + part
            at = pl.ds(part * SROWS, SROWS)
            gate = jnp.zeros((SROWS, 128), F32)
            for n in range(SET):
                one = gr[s * SET + n].astype(F32)[0:1, :]
                gate = jnp.where(in_place & (source_at == n), one, gate)
            g = jnp.sum(gate, axis=1, keepdims=True)
            a, b, u = acc[0, at], acc[1, at], acc[2, at]
            sig = jax.nn.sigmoid(a)
            silu = a * sig
            hidden = silu * b
            dh = g * u
            pool[0 * SETS + s] = (dh * b * sig * (1.0 + a * (1.0 - sig))).astype(BF16)
            pool[1 * SETS + s] = (dh * silu).astype(BF16)
            pool[2 * SETS + s] = (g * hidden).astype(BF16)
            q = jnp.sum(u * hidden, axis=1, keepdims=True)
            for n in range(SET):
                mine = jnp.where(in_place & (source_at == n), q, 0.0)
                qp[s, pl.ds(n, 1), :] = jnp.sum(mine, axis=0, keepdims=True)

        @pl.when(i > 1)
        def _():
            for copy in s1_copies(i - 2):
                copy.wait_send()

        s1s[i % 2, 0] = partial(i, opp, 0)
        s1s[i % 2, 1] = partial(i, opp, 1)
        for copy in s1_copies(i):
            copy.start()

        @pl.loop(0, 2)
        def _(h):
            s2s[i, 0, 1 - h] = partial(i, right, 1 - h)
            s2s[i, 1, h] = partial(i, left, h)

            @pl.when(h == 0)
            def _():
                for copy in d_copies(i):
                    copy.start()

            own[i % 3, h] = partial(i, th, h)

        @pl.when(i > 0)
        def _():
            combine(i - 1)

        @pl.when(i > 1)
        def _():
            finish(i - 2)

    q_copies = tuple(
        th_copy(qp, qr.at[n], q_s.at[n], q_r.at[n], p) for n, p in enumerate((right, left, opp))
    )
    for copy in q_copies:
        copy.start()

    tile = half // 128

    def out_copies(t):
        return tuple(
            pltpu.make_async_copy(
                bounce.at[t % 2, pl.ds(n * tile, tile)], gw_ref.at[n, pl.ds(t * tile, tile)],
                o_s.at[t % 2, n],
            )
            for n in range(3)
        )

    def weight_grads(t):
        @pl.when(t > 1)
        def _():
            for copy in out_copies(t - 2):
                copy.wait()

        span = pl.ds(pl.multiple_of(t % 2 * half, half), half)
        for n, kind in enumerate((0, 0, 1)):
            rows = xy[t // 2, :, kind, :, span].reshape(SETS * SROWS, half)
            hid = hidden_rows(n, 0, SETS)
            value = lax.dot_general(rows, hid, over_rows, preferred_element_type=F32)
            bounce[t % 2, pl.ds(n * tile, tile)] = value.astype(BF16).reshape(tile, 128, cols)
        for copy in out_copies(t):
            copy.start()

    pl.loop(0, 2)(weight_grads)
    combine(CHUNKS - 1)
    finish(CHUNKS - 2)
    pl.loop(2, 5)(weight_grads)

    for copy in q_copies:
        copy.wait_recv()

    def qb_copy(k):
        return ep_copy(gs.at[k], qb.at[k], qb_s.at[k], qb_r.at[k], peer_from(me, k))

    qb_own = pltpu.make_async_copy(gs.at[0], qb.at[0], qb_r.at[0])
    for s in range(SETS):
        total = qp[s] + qr[0, s] + qr[1, s] + qr[2, s]
        for n in range(SET):
            gs[s * SET + n] = jnp.broadcast_to(total[n : n + 1, :], (16, 128)).astype(BF16)
    qb_own.start()

    @pl.loop(1, PEERS)
    def _(k):
        qb_copy(k).start()

    def load(k):
        return pltpu.make_async_copy(back_ref.at[k], rr.at[k, :, pl.ds(strip, strip)], l_s.at[k])

    qb_own.wait()

    for m in range(2):
        sums[m] = jnp.zeros((pair, strip), F32)

    def sum_tokens(first, last):
        @pl.loop(first, last)
        def _(k):
            @pl.when(k > 0)
            def _():
                b_copy(k).wait_recv()

            @pl.when(k == 0)
            def _():
                b_own.wait()

            load(k).start()

        @pl.loop(first, last)
        def _(k):
            @pl.when(k > 0)
            def _():
                qb_copy(k).wait_recv()

            load(k).wait()
            chosen = one_hot(k)
            found = jnp.dot(qb[k], chosen[:128, :tok_count], preferred_element_type=F32)
            routed[pl.ds(k, 1), :] = found[0:1, :]
            for m in range(2):
                sums[m] += lax.dot_general(
                    chosen[:, m * pair : (m + 1) * pair], rr[k, :, pl.ds(strip, strip)], over_rows,
                    preferred_element_type=F32,
                )

    sum_tokens(0, PEERS - 2 * SET)
    finish(CHUNKS - 1)
    pl.loop(5, 8)(weight_grads)
    for t in (6, 7):
        for copy in out_copies(t):
            copy.wait()

    sum_tokens(PEERS - 2 * SET, PEERS)
    for c in range(4):
        tok_out[:, pl.ds(c * strip, strip)] = sums[
            c // 2, pl.ds(c % 2 * tok_count, tok_count)
        ].astype(BF16)
    terms = routed[...]
    for n in range(top_count):
        same = routing_ref[pl.ds(n, 1), :] == expert
        gates_out[pl.ds(n, 1), :] = jnp.sum(jnp.where(same, terms, 0.0), axis=0, keepdims=True)

    @pl.loop(1, PEERS)
    def _(k):
        b_copy(k).wait_send()
        qb_copy(k).wait_send()

    for copy in q_copies:
        copy.wait_send()

    @pl.loop(0, SETS)
    def _(i):
        for copy in (*z_copies(i), *v_copies(i)):
            copy.wait_send()

    @pl.loop(0, CHUNKS)
    def _(i):
        for copy in (*d_copies(i), *s2_copies(i)):
            copy.wait_send()

    for i in (CHUNKS - 2, CHUNKS - 1):
        for copy in s1_copies(i):
            copy.wait_send()


def local(tokens, cotangent, gates, routing, new_slot, gate_old, up_old, down_old):
    tok_count, top_count = routing.shape
    quarter = tokens.shape[1]
    depth, cols = gate_old.shape[1:]
    ids = jnp.arange(PEERS, dtype=jnp.int32)
    expert = peer_to(lax.axis_index("ep"), ids)
    order = jnp.sum(
        (new_slot[None, :] == expert[:, None]).astype(jnp.int32) * ids[None, :], axis=1
    )
    half = quarter // 2
    strip = quarter // 4
    dma = pltpu.SemaphoreType.DMA
    peer, three = dma((PEERS,)), dma((3, PEERS))
    sets, ring = dma((2, SETS)), dma((2, CHUNKS))
    anywhere = pl.BlockSpec(memory_space=pl.ANY)
    inside = pl.BlockSpec(memory_space=pltpu.VMEM)
    grads, _, grad_tokens, grad_gates = pl.pallas_call(
        layer_body,
        out_shape=[
            jax.ShapeDtypeStruct((3, PEERS, depth, cols), BF16),
            jax.ShapeDtypeStruct((PEERS, SROWS, strip), BF16),
            jax.ShapeDtypeStruct(tokens.shape, BF16),
            jax.ShapeDtypeStruct((top_count, tok_count), F32),
        ],
        in_specs=[pl.BlockSpec(memory_space=pltpu.SMEM)] + [inside] * 5 + [anywhere] * 3,
        out_specs=[anywhere] * 2 + [inside] * 2,
        scratch_shapes=[
            pltpu.VMEM((PEERS, 3 * depth, cols), BF16),
            pltpu.VMEM((4, SETS, 2, SROWS, quarter), BF16),
            pltpu.VMEM((PEERS, SROWS, half), BF16),
            pltpu.VMEM((PEERS, 16, 128), BF16),
            pltpu.VMEM((PEERS, 16, 128), BF16),
            pltpu.VMEM((3, CROWS, cols), F32),
            pltpu.VMEM((2, 2, CROWS, half), BF16),
            pltpu.VMEM((CHUNKS, 2, CROWS, half), BF16),
            pltpu.VMEM((CHUNKS, 2, 2, CROWS, half), BF16),
            pltpu.VMEM((CHUNKS, 2, 2, CROWS, half), BF16),
            pltpu.VMEM((3, 2, CROWS, half), BF16),
            pltpu.VMEM((SETS, 8, 128), F32),
            pltpu.VMEM((3, SETS, 8, 128), F32),
            pltpu.VMEM((PEERS, 16, 128), BF16),
            pltpu.VMEM((PEERS, SROWS, cols), BF16),
            pltpu.VMEM((2, PEERS, depth, cols), BF16),
            pltpu.VMEM((4, SROWS, SET * SROWS), BF16),
            pltpu.VMEM((2, 2 * tok_count, strip), F32),
            pltpu.VMEM((PEERS, 4 * tok_count), F32),
            pltpu.VMEM((PEERS, tok_count), F32),
            pltpu.VMEM((PEERS, tok_count), F32),
            peer, peer, peer, peer, three, three,
            sets, sets, sets, sets, ring, ring, ring, ring, ring, ring,
            peer, peer, dma((3,)), dma((3,)), peer, peer, dma((2, 3)), dma((3,)), peer,
        ],
        compiler_params=pltpu.CompilerParams(
            collective_id=0, has_side_effects=True, vmem_limit_bytes=63 * 2**20
        ),
    )(
        order, tokens, cotangent, gates.astype(F32).T, routing.T,
        jnp.broadcast_to(expert[:, None], (PEERS, tok_count)), gate_old, up_old, down_old,
    )
    grads = grads.reshape(3, PEERS * depth, cols)
    return (grad_tokens, grad_gates.T.astype(BF16), grads[0:1], grads[1:2], grads[2:3])


def solution(mesh):
    placed = (
        P("ep", "th"),
        P("ep", "th"),
        P("ep", None),
        P("ep", None),
        P(),
        P(None, "ep", "th"),
        P(None, "ep", "th"),
        P(None, "ep", "th"),
    )
    return jax.shard_map(
        local,
        mesh=mesh,
        in_specs=placed,
        out_specs=(
            P("ep", "th"),
            P("ep", None),
            P("ep", None, "th"),
            P("ep", None, "th"),
            P("ep", None, "th"),
        ),
        check_vma=False,
    )
```
